32 devices in a mesh: section: 2 (over x), dp: 16 (over z, y, core).
Axes of the slice: x: 2, y: 2, z: 4, core: 2. Of those that a mesh axis runs over, the one named last changes fastest.
Arguments:
- tokens: bfloat16 [16384, 768], P('dp'), may hold values from -6 to 6
- segment_ids: int32 [16384], P('dp'), may hold values from 0 to 511, as said below
- cotangent: bfloat16 [16384, 768], P('dp'), may hold values from -6 to 6
- norm_gains: float32 [2, 2, 768], P('section'), may hold values from 0.5 to 1.5
- mixing_table: bfloat16 [2, 12, 512, 512], P('section'), may hold values from -8 to 8
- value_weight: bfloat16 [2, 768, 768], P('section'), may hold values from -0.21875 to 0.21875
- out_weight: bfloat16 [2, 768, 768], P('section'), may hold values from -0.625 to 0.625
- up_weight: bfloat16 [2, 768, 3072], P('section'), may hold values from -0.21875 to 0.21875
- down_weight: bfloat16 [2, 3072, 768], P('section'), may hold values from -0.109375 to 0.109375
Outputs:
- layer_outputs: bfloat16 [2, 16384, 768], P('section', 'dp')
- stream_grads: float32 [2, 16384, 768], P('section', 'dp')
- gains_grad: float32 [2, 2, 768], P('section', None, 'dp')
- mixing_grad: float32 [2, 12, 512, 512], P('section', None, 'dp')
- value_grad: float32 [2, 768, 768], P('section', None, 'dp')
- out_grad: float32 [2, 768, 768], P('section', None, 'dp')
- up_grad: float32 [2, 768, 3072], P('section', None, 'dp')
- down_grad: float32 [2, 3072, 768], P('section', None, 'dp')
The draws below stay inside these ranges and needn't reach their ends.
Inputs may be any that keep to these rules, and one draw needn't show every extreme that they name: `segment_ids`: within each aligned row of 512 tokens, the id of a token is the position in its row of the first token of its document, so ids never fall within a row and start at 0; the last token of every row is a document of its own.
All inputs are finite; a program needn't handle non-finite values.
Results may differ from the reference program's by a relative error of at most 0.013.
Values may be sent and summed in bfloat16 or wider, within the bound.
No kernel may reach another device: no remote copies, remote signals or barrier semaphores. Data moves between devices by JAX's collectives and lax.ppermute only.
A program may use at most 256 MiB of HBM per device.

```python
import jax
import jax.numpy as jnp
from jax import lax

D = 768
H = 12
HD = 64
FF = 3072
L = 512
SEQ_MB = 1
MICRO = 2
TOKENS = 16384


def draw_segment_ids(key, part):
    key = jax.random.fold_in(key, 7)
    coins = jax.random.randint(key, (TOKENS,), 0, 40)
    position = jnp.arange(TOKENS, dtype=jnp.int32) % L
    begins = (coins == 0) | (position == 0) | (position == L - 1)
    marked = jnp.where(begins, position, 0).reshape(TOKENS // L, L)
    return lax.cummax(marked, axis=1).reshape(TOKENS).astype(jnp.int32)


def raised(values, key, source, target, shards_of, factor):
    def block_of(dim):
        return (jnp.arange(values.shape[dim]) // (values.shape[dim] // shards_of)).reshape((-1,) + (1,) * (values.ndim - 1 - dim))

    near = jax.random.permutation(key, shards_of)[block_of(target)]
    far = (block_of(target) + shards_of // 2) % shards_of
    return jnp.where((block_of(source) == near) | (block_of(source) == far), factor * values, values)


def steps_of(own_key, shape, cuts, low, largest):
    def one(axis_at, parts):
        steps = jax.random.uniform(jax.random.fold_in(jax.random.fold_in(own_key, 6), axis_at), (parts,), jnp.float32, low / len(cuts), largest / len(cuts))
        return jnp.repeat(jnp.exp(steps), shape[axis_at] // parts).reshape((-1,) + (1,) * (len(shape) - axis_at - 1))

    level = one(*cuts[0])
    for cut in cuts[1:]:
        level = level * one(*cut)
    return level


def gaussian(rng, dims, spread, reach, cuts=(), held_as=jnp.bfloat16):
    values = spread * jax.random.normal(rng, dims, jnp.float32)
    if cuts:
        values = values * steps_of(rng, dims, cuts, -0.22, 0.18)
    return jnp.clip(values, -reach, reach).astype(held_as)


def bell_draw_with(key, shape, scale, limit, shards, heavy, kind=jnp.bfloat16):
    values = scale * jax.random.normal(key, shape, jnp.float32)
    if shards:
        values = values * steps_of(key, shape, shards, -0.22, 0.18)
    return jnp.clip(raised(values, jax.random.fold_in(key, 3), *heavy), -limit, limit).astype(kind)


def setup_inputs(seed: int = 0) -> dict:
    keys = jax.random.split(jax.random.key(seed), 10)
    tokens = gaussian(keys[0], (TOKENS, D), 1.0, 6.0, ((0, 16),))
    segment_ids = draw_segment_ids(jax.random.fold_in(keys[9], 71), 0)
    cotangent = bell_draw_with(keys[2], (TOKENS, D), 1.0, 6.0, ((0, 16),), (0, 1, 16, 2.0))
    norm_gains = jnp.clip(1.0 + 0.1 * jax.random.normal(keys[3], (2, 2, D), jnp.float32), 0.5, 1.5)
    mixing_table = gaussian(keys[4], (2, H, L, L), 1.5, 8.0, ((0, 2),))
    value_weight = gaussian(keys[5], (2, D, D), D ** -0.5, 0.21875, ((0, 2),))
    out_weight = gaussian(keys[6], (2, D, D), (D // 8) ** -0.5, 0.625, ((0, 2),))
    up_weight = gaussian(keys[7], (2, D, FF), D ** -0.5, 0.21875, ((0, 2),))
    down_weight = gaussian(keys[8], (2, FF, D), FF ** -0.5, 0.109375, ((0, 2),))
    return {"tokens": tokens, "segment_ids": segment_ids, "cotangent": cotangent, "norm_gains": norm_gains, "mixing_table": mixing_table, "value_weight": value_weight, "out_weight": out_weight, "up_weight": up_weight, "down_weight": down_weight}


@jax.custom_vjp
def low(v):
    return lax.optimization_barrier(v.astype(jnp.bfloat16)).astype(jnp.float32)

@jax.custom_vjp
def low_back(v):
    return v

def low_keep(v):
    return (low(v), None)

def low_pass(kept, grad):
    return (grad,)

def back_keep(v):
    return (v, None)

def back_low(kept, grad):
    return (low(grad),)
low.defvjp(low_keep, low_pass)
low_back.defvjp(back_keep, back_low)
eps_norm = 1e-06
highest = lax.Precision.HIGHEST

def rms_norm(values, gain):
    return values * lax.rsqrt(lax.optimization_barrier(jnp.mean(values * values, axis=-1, keepdims=True)) + eps_norm) * gain

def layer(stream_in, seg_ids, gain_pair, mix_table, w_value, w_out, w_up, w_down, causal):
    normed_one = low(rms_norm(stream_in, gain_pair[0]))
    values_low = low(low_back(jnp.dot(normed_one, w_value, precision=highest)))
    row_count = stream_in.shape[0] // L
    block_seqs = SEQ_MB * MICRO
    block_count = row_count // block_seqs
    value_blocks = values_low.reshape(block_count, block_seqs, L, H, HD)
    seg_blocks = seg_ids.reshape(block_count, block_seqs, L)
    row_pos = lax.broadcasted_iota(jnp.int32, (L, L), 0)
    col_pos = lax.broadcasted_iota(jnp.int32, (L, L), 1)

    def mix_block(pieces):
        block_values, block_seg = pieces
        allowed = block_seg[:, :, None] == block_seg[:, None, :]
        if causal:
            allowed = allowed & (col_pos <= row_pos)[None]
        scores = jnp.where(allowed[:, None], mix_table[None], -1e+30)
        prob_full = jax.nn.softmax(scores, axis=-1)
        return jnp.einsum('shij,sjhd->sihd', low(prob_full), block_values, precision=highest)
    mixed = lax.map(jax.checkpoint(mix_block), (value_blocks, seg_blocks)).reshape(stream_in.shape)
    mixed_low = low(low_back(mixed))
    residual_mid = stream_in + low_back(jnp.dot(mixed_low, w_out, precision=highest))
    normed_two = low(rms_norm(residual_mid, gain_pair[1]))
    pre_act = low_back(jnp.dot(normed_two, w_up, precision=highest))
    act_low = low(jax.nn.gelu(pre_act))
    return residual_mid + low_back(jnp.dot(act_low, w_down, precision=highest))

def reference(tokens, segment_ids, cotangent, norm_gains, mixing_table, value_weight, out_weight, up_weight, down_weight):
    stream_in = tokens.astype(jnp.float32)
    params = (norm_gains.astype(jnp.float32), mixing_table.astype(jnp.float32), value_weight.astype(jnp.float32), out_weight.astype(jnp.float32), up_weight.astype(jnp.float32), down_weight.astype(jnp.float32))
    probe = jnp.zeros(stream_in.shape, jnp.float32)

    def forward(stream_in, params, probe):
        gains, tables, values, outs, ups, downs = params
        encoded = layer(stream_in, segment_ids, gains[0], tables[0], values[0], outs[0], ups[0], downs[0], False)
        middle = low(low_back(encoded)) + probe
        decoded = layer(middle, segment_ids, gains[1], tables[1], values[1], outs[1], ups[1], downs[1], True)
        return (encoded, decoded)
    (encoded, decoded), backward = jax.vjp(forward, stream_in, params, probe)
    grad_in, grad_params, grad_probe = backward((jnp.zeros(encoded.shape, jnp.float32), cotangent.astype(jnp.float32)))
    both_out = jnp.stack([encoded, decoded]).astype(jnp.bfloat16)
    both_grads = jnp.stack([grad_in, grad_probe])
    return (both_out, both_grads, grad_params[0], grad_params[1], grad_params[2], grad_params[3], grad_params[4], grad_params[5])
```

```python
import jax
import jax.numpy as jnp
from jax import lax
from jax.sharding import PartitionSpec as P

L = 512
HD = 64
eps_norm = 1e-06
bf16 = jnp.bfloat16
f32 = jnp.float32
K0 = 0.7978845608028654
K1 = 0.044715


def dot(a, b, ca, cb):
    return lax.dot_general(a, b, (((ca,), (cb,)), ((), ())), preferred_element_type=f32)


def rms_scale(values):
    return lax.rsqrt(jnp.mean(values * values, axis=-1, keepdims=True) + eps_norm)


def gelu_parts(u):
    t = jnp.tanh(K0 * (u + K1 * u * u * u))
    z = 0.5 * u * (1.0 + t)
    g = 0.5 * (1.0 + t) + 0.5 * u * (1.0 - t * t) * (K0 * (1.0 + 3.0 * K1 * u * u))
    return z, g


def forward_row(x, mask, expo, weights):
    gains, w_value, w_out, w_up, w_down = weights
    heads = expo.shape[0]
    length, width = x.shape
    xf = x.astype(f32)
    s1 = rms_scale(xf)
    a1 = (xf * s1 * gains[0]).astype(bf16)
    v = dot(a1, w_value, 1, 0).astype(bf16)
    em = expo * mask[None]
    inv = 1.0 / jnp.sum(em.astype(f32), axis=-1)
    vh = v.reshape(length, heads, HD)
    o = jnp.einsum("hij,jhd->ihd", em, vh, preferred_element_type=f32) * inv.T[:, :, None]
    o = o.astype(bf16).reshape(length, width)
    m = xf + dot(o, w_out, 1, 0)
    s2 = rms_scale(m)
    a2 = (m * s2 * gains[1]).astype(bf16)
    u = dot(a2, w_up, 1, 0)
    z, g = gelu_parts(u)
    z = z.astype(bf16)
    y = (m + dot(z, w_down, 1, 0)).astype(bf16)
    return y, (x, a1, v, inv, o, m, a2, z, g.astype(bf16))


def norm_back(grad, values, gain):
    s = rms_scale(values)
    hat = values * s
    scaled = grad * gain
    back = s * (scaled - hat * jnp.mean(scaled * hat, axis=-1, keepdims=True))
    return back, jnp.sum(grad * hat, axis=0)


def backward_row(dy, res, mask, expo, weights):
    gains, w_value, w_out, w_up, w_down = weights
    x, a1, v, inv, o, m, a2, z, g = res
    heads = expo.shape[0]
    length, width = x.shape
    dz = dot(dy, w_down, 1, 1)
    du = (dz * g.astype(f32)).astype(bf16)
    da2 = dot(du, w_up, 1, 1)
    back2, dg2 = norm_back(da2, m, gains[1])
    dm = dy.astype(f32) + back2
    dml = dm.astype(bf16)
    do = dot(dml, w_out, 1, 1).reshape(length, heads, HD)
    don = (do * inv.T[:, :, None]).astype(bf16)
    em = expo * mask[None]
    dv = jnp.einsum("hij,ihd->jhd", em, don, preferred_element_type=f32)
    dv = dv.reshape(length, width).astype(bf16)
    da1 = dot(dv, w_value, 1, 1)
    back1, dg1 = norm_back(da1, x.astype(f32), gains[0])
    dx = dm + back1
    return dx, (du, dml, don, dv, jnp.stack([dg1, dg2]))


def mixing_row(don, o, v, mask, expo):
    heads = expo.shape[0]
    length = don.shape[0]
    oh = o.reshape(length, heads, HD)
    vh = v.reshape(length, heads, HD)
    delta = jnp.sum(don.astype(f32) * oh.astype(f32), axis=-1).T
    dp = jnp.einsum("ihd,jhd->hij", don, vh, preferred_element_type=f32)
    return (expo * mask[None]).astype(f32) * (dp - delta[:, :, None])


def ring_groups(size):
    zs = size // 4
    return [
        [(z * 2) * 2 + c for z in range(zs)] + [((zs - 1 - z) * 2 + 1) * 2 + c for z in range(zs)]
        for c in range(2)
    ]


def scatter_sum(grad, size):
    rest = grad.shape[1:]
    core = lax.axis_index("dp") % 2
    zs = size // 4
    by = grad.reshape((zs, 2, 2) + rest)
    ring = jnp.concatenate([by[:, 0], by[::-1, 1]], axis=0)
    keep = lax.dynamic_index_in_dim(ring, core, 1, False)
    send = lax.dynamic_index_in_dim(ring, 1 - core, 1, False)
    got = lax.ppermute(send, "dp", [(d, d ^ 1) for d in range(size)])
    total = keep + got
    out = lax.psum_scatter(
        total, "dp", scatter_dimension=0, tiled=True, axis_index_groups=ring_groups(size)
    )
    return out.reshape(rest)


def shards(tokens, segment_ids, cotangent, norm_gains, mixing, w_value, w_out, w_up, w_down):
    size = lax.axis_size("dp")
    is_enc = lax.axis_index("section") == 0
    rows = tokens.shape[0] // L
    weights = (norm_gains[0], w_value[0], w_out[0], w_up[0], w_down[0])
    expo = jnp.exp(mixing[0].astype(f32)).astype(bf16)
    seg = segment_ids.reshape(rows, L)
    pos = lax.broadcasted_iota(jnp.int32, (L, L), 0)
    key = lax.broadcasted_iota(jnp.int32, (L, L), 1)
    masks = [
        ((seg[r][:, None] == seg[r][None, :]) & ((key <= pos) | is_enc)).astype(bf16)
        for r in range(rows)
    ]
    tok = [tokens[r * L : (r + 1) * L] for r in range(rows)]
    cot = [cotangent[r * L : (r + 1) * L] for r in range(rows)]
    sent = []
    for r in range(rows):
        y, _ = forward_row(tok[r], masks[r], expo, weights)
        sent.append(lax.ppermute(y, "section", [(0, 1)]))
    ys, saved, back = [], [], []
    for r in range(rows):
        x = jnp.where(is_enc, tok[r], sent[r])
        y, res = forward_row(x, masks[r], expo, weights)
        ys.append(y)
        saved.append(res)
        dx, _ = backward_row(cot[r], res, masks[r], expo, weights)
        back.append(lax.ppermute(dx.astype(bf16), "section", [(1, 0)]))
    dxs, grads, dys = [], [], []
    mix = 0.0
    gains = 0.0
    for r in range(rows):
        dy = jnp.where(is_enc, back[r], cot[r])
        dx, got = backward_row(dy, saved[r], masks[r], expo, weights)
        dys.append(dy)
        dxs.append(dx)
        grads.append(got)
        mix = mix + mixing_row(got[2], saved[r][4], saved[r][2], masks[r], expo)
        gains = gains + got[4]

    def cat(pieces):
        return jnp.concatenate(pieces, axis=0)

    z = cat([s[7] for s in saved])
    a2 = cat([s[6] for s in saved])
    o = cat([s[4] for s in saved])
    a1 = cat([s[1] for s in saved])
    heads = expo.shape[0]
    width = tokens.shape[1]
    down_t = dot(cat(dys), z, 0, 0).astype(bf16).reshape(size, -1, z.shape[1])
    up_t = dot(cat([g[0] for g in grads]), a2, 0, 0).astype(bf16).reshape(size, -1, width)
    out_t = dot(cat([g[1] for g in grads]), o, 0, 0).astype(bf16).reshape(size, -1, width)
    value_t = dot(cat([g[3] for g in grads]), a1, 0, 0).astype(bf16).reshape(size, -1, width)
    mix_t = mix.astype(bf16).reshape(heads, size, L // size, L).transpose(1, 0, 2, 3)
    gain_t = gains.astype(bf16).reshape(2, size, -1).transpose(1, 0, 2).reshape(size, 1, -1)
    gain_t = jnp.pad(gain_t, ((0, 0), (0, 15), (0, width - gain_t.shape[2])))
    per = width // size
    down_g = scatter_sum(down_t, size).astype(f32).T
    up_g = scatter_sum(up_t, size).astype(f32).T
    mix_g = scatter_sum(mix_t, size).astype(f32)
    small = scatter_sum(jnp.concatenate([out_t, value_t, gain_t], axis=1), size).astype(f32)
    out_g = small[:per].T
    value_g = small[per : 2 * per].T
    gains_g = small[2 * per, : 2 * per].reshape(2, per)
    return (
        cat(ys)[None],
        cat(dxs)[None],
        gains_g[None],
        mix_g[None],
        value_g[None],
        out_g[None],
        up_g[None],
        down_g[None],
    )


def solution(mesh):
    placed = (
        P("dp", None),
        P("dp"),
        P("dp", None),
        P("section", None, None),
        P("section", None, None, None),
        P("section", None, None),
        P("section", None, None),
        P("section", None, None),
        P("section", None, None),
    )
    return jax.shard_map(
        shards,
        mesh=mesh,
        in_specs=placed,
        out_specs=(
            P("section", "dp", None),
            P("section", "dp", None),
            P("section", None, "dp"),
            P("section", None, "dp", None),
            P("section", None, "dp"),
            P("section", None, "dp"),
            P("section", None, "dp"),
            P("section", None, "dp"),
        ),
        check_vma=False,
    )
```

```python
import functools
import jax
import jax.numpy as jnp
from jax import lax
from jax.experimental import pallas as pl
from jax.experimental.pallas import tpu as pltpu
from jax.sharding import PartitionSpec as P

L = 512
HD = 64
eps_norm = 1e-06
bf16 = jnp.bfloat16
f32 = jnp.float32
C0 = 0.7978845608028654
C1 = C0 * 0.044715
RC = 128
MIB = 1024 * 1024
ANY = pl.BlockSpec(memory_space=pl.ANY)
WHOLE = pl.BlockSpec(memory_space=pltpu.VMEM)
SMEM = pl.BlockSpec(memory_space=pltpu.SMEM)
sds = jax.ShapeDtypeStruct


def dot(a, b, ca, cb):
    return lax.dot_general(a, b, (((ca,), (cb,)), ((), ())), preferred_element_type=f32)


def rms_scale(values):
    return lax.rsqrt(jnp.mean(values * values, axis=-1, keepdims=True) + eps_norm)


def gelu_parts(u, want_slope):
    w = u * u
    h = 0.5 + 0.5 * jnp.tanh(u * (C0 + C1 * w))
    if not want_slope:
        return u * h, None
    slope = u * (C0 + (3.0 * C1) * w)
    return u * h, h + (h - h * h) * (slope + slope)


def build_mask(seg, is_enc, mask_ref):
    across = jnp.broadcast_to(seg, (128, L)).T
    for b in range(L // 128):
        same = across == seg[:, b * 128 : (b + 1) * 128]
        pos = lax.broadcasted_iota(jnp.int32, (L, 128), 0)
        key = lax.broadcasted_iota(jnp.int32, (L, 128), 1) + b * 128
        seen = (key <= pos) | (is_enc == 1)
        mask_ref[:, b * 128 : (b + 1) * 128] = jnp.where(same & seen, 1.0, 0.0).astype(bf16)


class Copies:
    def __init__(self, sems):
        self.sems = sems
        self.all = []

    def start(self, src, dst):
        copy = pltpu.make_async_copy(src, dst, self.sems.at[len(self.all)])
        copy.start()
        self.all.append(copy)
        return copy

    def wait(self):
        for copy in self.all:
            copy.wait()


def forward_kernel(first, full, row, *refs):
    it = iter(refs)
    take = lambda n: [next(it) for _ in range(n)]
    flag, seg, gains, tok = take(4)
    recv = next(it) if full else None
    src = take(5)
    y_out = next(it)
    if first:
        table, wv, wo, wu, wd = take(5)
    else:
        table, wv, wo, wu, wd = src
    res = dict(zip(RES, take(len(RES)))) if full else {}
    xb, mask, a1b, vb, ob, mb, a2b, yb = take(8)
    if full:
        rb, invb, zb, gb = take(4)
    sin, sout = take(2)
    heads, width, ff = table.shape[0], tok.shape[1], wu.shape[1]
    pairs, nf = heads // 2, ff // width
    ins, outs = Copies(sin), Copies(sout)

    def save(name, src_ref, *where):
        if full:
            dst = res[name]
            outs.start(src_ref, dst.at[where] if where else dst)

    cx = ins.start(tok.at[pl.ds(row * L, L)], xb)
    if full:
        cr = ins.start(recv, rb)
    if first:
        cv = ins.start(src[1], wv)
        ct = [ins.start(src[0].at[pl.ds(2 * p, 2)], table.at[pl.ds(2 * p, 2)]) for p in range(pairs)]
        co = ins.start(src[2], wo)
        cu = [ins.start(src[3].at[:, pl.ds(k * width, width)], wu.at[:, pl.ds(k * width, width)]) for k in range(nf)]
        cd = [ins.start(src[4].at[pl.ds(k * width, width)], wd.at[pl.ds(k * width, width)]) for k in range(nf)]
    is_enc = flag[0]
    build_mask(seg[row : row + 1, :].astype(f32), is_enc, mask)
    cx.wait()
    if full:
        cr.wait()
        xb[...] = jnp.where(is_enc == 1, xb[...], rb[...])
        save("x", xb)
    for c in range(L // RC):
        rows = slice(c * RC, (c + 1) * RC)
        xf = xb[rows, :].astype(f32)
        a1b[rows, :] = (xf * rms_scale(xf) * gains[0:1, :]).astype(bf16)
    if first:
        cv.wait()
    vb[...] = dot(a1b[...], wv[...], 1, 0).astype(bf16)
    save("a1", a1b)
    save("v", vb)
    low = lax.broadcasted_iota(jnp.int32, (L, 128), 1) < HD
    one = jnp.ones((L, 128), bf16)
    for p in range(pairs):
        cols = slice(p * 128, (p + 1) * 128)
        if first:
            ct[p].wait()
            for h in (2 * p, 2 * p + 1):
                table[h] = jnp.exp(table[h].astype(f32)).astype(bf16)
        vp = vb[:, cols]
        even = dot(table[2 * p] * mask[...], jnp.where(low, vp, one), 1, 0)
        odd = dot(table[2 * p + 1] * mask[...], jnp.where(low, one, vp), 1, 0)
        inv = 1.0 / pltpu.roll(jnp.where(low, odd, even), HD, 1)
        ob[:, cols] = (jnp.where(low, even, odd) * inv).astype(bf16)
        if full:
            invb[:, cols] = inv
    save("o", ob)
    if full:
        save("inv", invb)
    if first:
        co.wait()
    mb[...] = xb[...].astype(f32) + dot(ob[...], wo[...], 1, 0)
    save("m", mb)
    for c in range(L // RC):
        rows = slice(c * RC, (c + 1) * RC)
        m = mb[rows, :]
        a2b[rows, :] = (m * rms_scale(m) * gains[1:2, :]).astype(bf16)
    save("a2", a2b)
    acc = mb[...]
    u = None
    for k in range(nf + 1):
        if k < nf:
            if first:
                cu[k].wait()
            following = dot(a2b[...], wu[:, k * width : (k + 1) * width], 1, 0)
        if k > 0:
            cols = slice((k - 1) * width, k * width)
            z, g = gelu_parts(u, full)
            z = z.astype(bf16)
            if full:
                zb[:, cols] = z
                gb[:, cols] = g.astype(bf16)
                part = (slice(None), pl.ds((k - 1) * width, width))
                save("z", zb.at[part], *part)
                save("g", gb.at[part], *part)
            if first:
                cd[k - 1].wait()
            acc = acc + dot(z, wd[cols, :], 1, 0)
        u = following
    yb[...] = acc.astype(bf16)
    outs.start(yb, y_out)
    outs.wait()


RES = ("x", "a1", "v", "inv", "o", "m", "a2", "z", "g")


def hold(arrays):
    return [pltpu.with_memory_space_constraint(a, pltpu.VMEM) for a in arrays]


def far(arrays):
    return [pltpu.with_memory_space_constraint(a, pltpu.HBM) for a in arrays]


def forward_row(row, flag, seg, gains, tok, recv, weights, first=False):
    full = recv is not None
    width, ff, heads = tok.shape[1], weights[3].shape[1], weights[0].shape[0]
    V = pltpu.VMEM
    wide = lambda dt: pltpu.HBM((L, width), dt)
    out_shape, out_specs = [wide(bf16)], [ANY]
    if first:
        out_shape += [V(w.shape, w.dtype) for w in weights]
        out_specs += [WHOLE] * 5
    if full:
        out_shape += [wide(bf16), wide(bf16), wide(bf16), wide(f32), wide(bf16), wide(f32), wide(bf16)]
        out_shape += [pltpu.HBM((L, ff), bf16)] * 2
        out_specs += [ANY] * len(RES)
    one = V((L, width), bf16)
    scratch = [one, V((L, L), bf16), one, one, one, V((L, width), f32), one, one]
    if full:
        scratch += [one, V((L, width), f32), V((L, ff), bf16), V((L, ff), bf16)]
    scratch += [pltpu.SemaphoreType.DMA((24,)), pltpu.SemaphoreType.DMA((24,))]
    ins = [flag, seg, gains, *far([tok] + ([recv] if full else [])), *(far(weights) if first else hold(weights))]
    specs = [SMEM, WHOLE, WHOLE] + [ANY] * (2 if full else 1) + [ANY if first else WHOLE] * 5
    macs = L * width * (2 * width + 2 * ff) + 2 * heads * L * L * 128
    got = pl.pallas_call(
        functools.partial(forward_kernel, first, full, row),
        out_shape=out_shape,
        in_specs=specs,
        out_specs=out_specs,
        scratch_shapes=scratch,
        compiler_params=pltpu.CompilerParams(vmem_limit_bytes=(30 if full else 20) * MIB),
        cost_estimate=pl.CostEstimate(flops=2 * macs, bytes_accessed=20_000_000, transcendentals=0),
    )(*ins)
    if first:
        return got[0], got[1:6]
    if full:
        return got[0], dict(zip(RES, got[1:]))
    return got[0]


def norm_back(grad, values, gain):
    scale = rms_scale(values)
    hat = values * scale
    scaled = grad * gain
    back = scale * (scaled - hat * jnp.mean(scaled * hat, axis=-1, keepdims=True))
    return back, jnp.sum(grad * hat, axis=0, keepdims=True)


def backward_kernel(full, row, *refs):
    it = iter(refs)
    take = lambda n: [next(it) for _ in range(n)]
    flag, seg, gains, cot = take(4)
    recv = next(it) if full else None
    table, wv, wo, wu, wd, x, inv, m, g = take(9)
    dx_out = next(it)
    if full:
        dy_out, du_out, dml_out, don_out, dvt_out, dg_out = take(6)
    dyb, mask, gb, mb, invb, xb, accb, dmlb, donb, dvtb, dxb = take(11)
    if full:
        rb, dub = take(2)
    sin, sout = take(2)
    heads, width, ff = table.shape[0], cot.shape[1], wu.shape[1]
    pairs, nf = heads // 2, ff // width
    ins, outs = Copies(sin), Copies(sout)
    cy = ins.start(cot.at[pl.ds(row * L, L)], dyb)
    if full:
        cr = ins.start(recv, rb)
    cg = []
    for k in range(nf):
        part = (slice(None), pl.ds(k * width, width))
        cg.append(ins.start(g.at[part], gb.at[part]))
    cm, ci, cx = ins.start(m, mb), ins.start(inv, invb), ins.start(x, xb)
    is_enc = flag[0]
    build_mask(seg[row : row + 1, :].astype(f32), is_enc, mask)
    cy.wait()
    if full:
        cr.wait()
        dyb[...] = jnp.where(is_enc == 1, rb[...], dyb[...])
        outs.start(dyb, dy_out)
    acc = None
    dz = None
    for k in range(nf + 1):
        if k < nf:
            following = dot(dyb[...], wd[k * width : (k + 1) * width, :], 1, 1)
        if k > 0:
            cols = slice((k - 1) * width, k * width)
            cg[k - 1].wait()
            du = (dz * gb[:, cols].astype(f32)).astype(bf16)
            if full:
                dub[:, cols] = du
                part = (slice(None), pl.ds((k - 1) * width, width))
                outs.start(dub.at[part], du_out.at[part])
            more = dot(du, wu[:, cols], 1, 1)
            acc = more if acc is None else acc + more
        dz = following
    accb[...] = acc
    cm.wait()
    dg2 = 0.0
    for c in range(L // RC):
        rows = slice(c * RC, (c + 1) * RC)
        back, dg = norm_back(accb[rows, :], mb[rows, :], gains[1:2, :])
        dg2 = dg2 + dg
        dm = dyb[rows, :].astype(f32) + back
        mb[rows, :] = dm
        dmlb[rows, :] = dm.astype(bf16)
    if full:
        outs.start(dmlb, dml_out)
    ci.wait()
    donb[...] = (dot(dmlb[...], wo[...], 1, 1) * invb[...]).astype(bf16)
    if full:
        outs.start(donb, don_out)
    for p in range(pairs):
        turned = donb[:, p * 128 : (p + 1) * 128].T
        for e in range(2):
            part = dot(turned[e * HD : (e + 1) * HD], table[2 * p + e] * mask[...], 1, 0)
            at = p * 128 + e * HD
            dvtb[at : at + HD, :] = part.astype(bf16)
    if full:
        outs.start(dvtb, dvt_out)
    accb[...] = dot(dvtb[...], wv[...], 0, 1)
    cx.wait()
    dg1 = 0.0
    for c in range(L // RC):
        rows = slice(c * RC, (c + 1) * RC)
        back, dg = norm_back(accb[rows, :], xb[rows, :].astype(f32), gains[0:1, :])
        dg1 = dg1 + dg
        dxb[rows, :] = (mb[rows, :] + back).astype(dxb.dtype)
    outs.start(dxb, dx_out)
    if full:
        dg_out[0:1, :] = dg1
        dg_out[1:2, :] = dg2
    outs.wait()


def backward_row(row, flag, seg, gains, cot, recv, weights, res):
    full = recv is not None
    width, ff, heads = cot.shape[1], weights[3].shape[1], weights[0].shape[0]
    V = pltpu.VMEM
    wide = lambda dt: pltpu.HBM((L, width), dt)
    dx_type = f32 if full else bf16
    out_shape, out_specs = [wide(dx_type)], [ANY]
    if full:
        out_shape += [wide(bf16), pltpu.HBM((L, ff), bf16), wide(bf16), wide(bf16), pltpu.HBM((width, L), bf16), sds((2, width), f32)]
        out_specs += [ANY] * 5 + [WHOLE]
    one = V((L, width), bf16)
    big = V((L, width), f32)
    scratch = [one, V((L, L), bf16), V((L, ff), bf16), big, big, one, big, one, one, V((width, L), bf16), V((L, width), dx_type)]
    if full:
        scratch += [one, V((L, ff), bf16)]
    scratch += [pltpu.SemaphoreType.DMA((16,)), pltpu.SemaphoreType.DMA((16,))]
    ins = [flag, seg, gains, *far([cot] + ([recv] if full else [])), *hold(weights), *far([res[n] for n in ("x", "inv", "m", "g")])]
    specs = [SMEM, WHOLE, WHOLE] + [ANY] * (2 if full else 1) + [WHOLE] * 5 + [ANY] * 4
    macs = L * width * (2 * width + 2 * ff) + 2 * heads * L * L * 64
    got = pl.pallas_call(
        functools.partial(backward_kernel, full, row),
        out_shape=out_shape,
        in_specs=specs,
        out_specs=out_specs,
        scratch_shapes=scratch,
        compiler_params=pltpu.CompilerParams(vmem_limit_bytes=(36 if full else 30) * MIB),
        cost_estimate=pl.CostEstimate(flops=2 * macs, bytes_accessed=20_000_000, transcendentals=0),
    )(*ins)
    if full:
        return got[0], dict(zip(("dy", "du", "dml", "don", "dvt", "dg"), got[1:]))
    return got[0]


def ring_place(zy, zs):
    z, y = zy // 2, zy % 2
    return z if y == 0 else 2 * zs - 1 - z


def put_halves(core, block, keep, send, at):
    half = block.shape[0] // 2
    top, bottom = block[:half], block[half:]
    keep[at] = jnp.where(core == 0, top, bottom).astype(keep.dtype)
    send[at] = jnp.where(core == 0, bottom, top).astype(send.dtype)


def load_both(copies, pieces, dst, axis):
    size = pieces[0].shape[axis]
    got = []
    for r, piece in enumerate(pieces):
        where = pl.ds(r * size, size)
        got.append(copies.start(piece, dst.at[where] if axis == 0 else dst.at[:, where]))
    return got


def up_kernel(rows, zs, *refs):
    flag = refs[0]
    du, a2 = refs[1 : 1 + rows], refs[1 + rows : 1 + 2 * rows]
    outs = refs[1 + 2 * rows : -3]
    dub, a2b, sem = refs[-3:]
    ins = Copies(sem)
    width, ff = a2b.shape[1], dub.shape[1]
    ca = load_both(ins, a2, a2b, 0)
    step = 768 if zs is None else ff // (2 * zs)
    cs = []
    for k in range(ff // 768):
        part = pl.ds(k * 768, 768)
        cs.append([ins.start(d.at[:, part], dub.at[pl.ds(r * L, L), part]) for r, d in enumerate(du)])
    for c in ca:
        c.wait()
    waited = 0
    for s in range(ff // step):
        while waited * 768 < (s + 1) * step:
            for c in cs[waited]:
                c.wait()
            waited += 1
        got = dot(dub[:, s * step : (s + 1) * step], a2b[...], 0, 0)
        if zs is None:
            outs[0][s * step : (s + 1) * step, :] = got.astype(outs[0].dtype)
        else:
            put_halves(flag[1], got, outs[0], outs[1], ring_place(s, zs))


def down_kernel(rows, zs, *refs):
    flag = refs[0]
    dy, z = refs[1 : 1 + rows], refs[1 + rows : 1 + 2 * rows]
    outs = refs[1 + 2 * rows : -3]
    dyb, zb, sem = refs[-3:]
    ins = Copies(sem)
    width, ff = dyb.shape[1], zb.shape[1]
    cy = load_both(ins, dy, dyb, 0)
    cs = []
    for k in range(ff // width):
        part = pl.ds(k * width, width)
        cs.append([ins.start(d.at[:, part], zb.at[pl.ds(r * L, L), part]) for r, d in enumerate(z)])
    for c in cy:
        c.wait()
    for k in range(ff // width):
        for c in cs[k]:
            c.wait()
        got = dot(dyb[...], zb[:, k * width : (k + 1) * width], 0, 0)
        if zs is None:
            outs[0][:, k * width : (k + 1) * width] = got.astype(outs[0].dtype)
            continue
        per = width // (4 * zs)
        for s in range(2 * zs):
            at = (ring_place(s, zs), slice(k * per, (k + 1) * per))
            put_halves(flag[1], got[2 * per * s : 2 * per * (s + 1)], outs[0], outs[1], at)


def small_kernel(rows, zs, *refs):
    flag, gain = refs[:2]
    take = lambda i: refs[2 + i * rows : 2 + (i + 1) * rows]
    dml, o, dvt, a1 = take(0), take(1), take(2), take(3)
    outs = refs[2 + 4 * rows : -5]
    dmlb, ob, dvtb, a1b, sem = refs[-5:]
    ins = Copies(sem)
    load_both(ins, dml, dmlb, 0)
    load_both(ins, o, ob, 0)
    load_both(ins, dvt, dvtb, 1)
    load_both(ins, a1, a1b, 0)
    width = ob.shape[1]
    for c in ins.all[: 2 * rows]:
        c.wait()
    for i in range(2):
        if i == 0:
            got = dot(dmlb[...], ob[...], 0, 0)
        else:
            for c in ins.all[2 * rows :]:
                c.wait()
            got = dot(dvtb[...], a1b[...], 1, 0)
        if zs is None:
            outs[i][...] = got.astype(outs[i].dtype)
            continue
        per = width // (4 * zs)
        for s in range(2 * zs):
            at = (ring_place(s, zs), slice(i * per, (i + 1) * per))
            put_halves(flag[1], got[2 * per * s : 2 * per * (s + 1)], outs[0], outs[1], at)
            if i == 0:
                wide = lambda d: jnp.broadcast_to(gain[d : d + 1, :], (16, width))
                both = jnp.concatenate([wide(2 * s), wide(2 * s + 1)], axis=0)
                at = (ring_place(s, zs), slice(2 * per, 2 * per + 16))
                put_halves(flag[1], both, outs[0], outs[1], at)


def mix_kernel(rows, zs, *refs):
    flag, seg, table = refs[:3]
    take = lambda i: refs[3 + i * rows : 3 + (i + 1) * rows]
    don, o, v = take(0), take(1), take(2)
    outs = refs[3 + 3 * rows : -1]
    mask = refs[-1]
    heads, width = table.shape[0], o[0].shape[1]
    is_enc, core = flag[0], flag[1]
    for r in range(rows):
        build_mask(seg[r : r + 1, :].astype(f32), is_enc, mask.at[r])
    lane = lax.broadcasted_iota(jnp.int32, (L, 128), 1)
    low = lane < HD
    one = jnp.ones((L, 128), bf16)
    for p in range(heads // 2):
        cols = slice(p * 128, (p + 1) * 128)
        total = [0.0, 0.0]
        for r in range(rows):
            dn, vp = don[r][:, cols], v[r][:, cols]
            prod = dn.astype(f32) * o[r][:, cols].astype(f32)
            for e in range(2):
                mine = low if e == 0 else ~low
                delta = jnp.sum(jnp.where(mine, prod, 0.0), axis=-1, keepdims=True) * (-1.0 / 32.0)
                high = delta.astype(bf16)
                rest = (delta - high.astype(f32)).astype(bf16)
                fill = jnp.where((lane & (HD - 1)) < 32, high, rest)
                left = jnp.where(mine, dn, fill)
                right = jnp.where(mine, vp, one)
                term = dot(left, right, 1, 1) * mask[r].astype(f32)
                total[e] = term if r == 0 else total[e] + term
        for e in range(2):
            h = 2 * p + e
            ds = total[e] * table[h].astype(f32)
            if zs is None:
                outs[0][h] = ds.astype(outs[0].dtype)
                continue
            per = L // (4 * zs)
            pieces = [(0, 0, 0, L)] if h % 3 == 0 else [(0, L, 0, L // 2), (1, 0, L // 2, L)] if h % 3 == 1 else [(1, L // 2, 0, L)]
            for s in range(2 * zs):
                block = ds[2 * per * s : 2 * per * (s + 1)]
                for strip, lane_at, a, b in pieces:
                    row_at = ((h // 3) * 2 + strip) * per
                    at = (ring_place(s, zs), slice(row_at, row_at + per), slice(lane_at, lane_at + b - a))
                    put_halves(core, block[:, a:b], outs[0], outs[1], at)


def weight_call(kernel, name, zs, shapes, plain, ins, specs, scratch, limit, macs):
    if zs is None:
        out_shape = [sds(s, f32) for s in plain]
    else:
        out_shape = [sds((2 * zs,) + shapes, bf16)] * 2
    return pl.pallas_call(
        kernel,
        out_shape=out_shape,
        in_specs=specs,
        out_specs=[WHOLE] * len(out_shape),
        scratch_shapes=scratch,
        compiler_params=pltpu.CompilerParams(vmem_limit_bytes=limit * MIB),
        cost_estimate=pl.CostEstimate(flops=2 * macs, bytes_accessed=12_000_000, transcendentals=0),
        name=name,
    )(*ins)


def up_grad(zs, flag, du, a2):
    rows, ff, width = len(du), du[0].shape[1], a2[0].shape[1]
    V = pltpu.VMEM
    return weight_call(
        functools.partial(up_kernel, rows, zs), "up_grad", zs,
        (ff // (4 * zs) if zs else 0, width), [(ff, width)],
        [flag, *far(du), *far(a2)], [SMEM] + [ANY] * (2 * rows),
        [V((rows * L, ff), bf16), V((rows * L, width), bf16), pltpu.SemaphoreType.DMA((16,))],
        36, rows * L * ff * width,
    )


def down_grad(zs, flag, dy, z):
    rows, ff, width = len(dy), z[0].shape[1], dy[0].shape[1]
    V = pltpu.VMEM
    return weight_call(
        functools.partial(down_kernel, rows, zs), "down_grad", zs,
        (ff // (4 * zs) if zs else 0, width), [(width, ff)],
        [flag, *far(dy), *far(z)], [SMEM] + [ANY] * (2 * rows),
        [V((rows * L, width), bf16), V((rows * L, ff), bf16), pltpu.SemaphoreType.DMA((16,))],
        36, rows * L * ff * width,
    )


def small_grad(zs, flag, gain, dml, o, dvt, a1):
    rows, width = len(dml), dml[0].shape[1]
    one = pltpu.VMEM((rows * L, width), bf16)
    return weight_call(
        functools.partial(small_kernel, rows, zs), "small_grad", zs,
        (width // (2 * zs) + 16 if zs else 0, width), [(width, width)] * 2,
        [flag, gain, *far(dml), *far(o), *far(dvt), *far(a1)], [SMEM, WHOLE] + [ANY] * (4 * rows),
        [one, one, pltpu.VMEM((width, rows * L), bf16), one, pltpu.SemaphoreType.DMA((16,))],
        30, 2 * rows * L * width * width,
    )


def mix_grad(zs, flag, seg, table, don, o, v):
    rows, width, heads = len(don), don[0].shape[1], table.shape[0]
    return weight_call(
        functools.partial(mix_kernel, rows, zs), "mix_grad", zs,
        (heads * L // (4 * zs) * L // width if zs else 0, width), [table.shape],
        [flag, seg, *hold([table]), *don, *o, *v], [SMEM, WHOLE, WHOLE] + [WHOLE] * (3 * rows),
        [pltpu.VMEM((rows, L, L), bf16)],
        36, rows * heads * L * L * 128,
    )


def rings(zs):
    order = sorted(range(2 * zs), key=lambda s: ring_place(s, zs))
    return [[2 * s + c for s in order] for c in range(2)]


def pair_sum(keep, send, size):
    return keep + lax.ppermute(send, "dp", [(d, d ^ 1) for d in range(size)])


def ring_sum(blocks, zs):
    total = lax.psum_scatter(blocks, "dp", scatter_dimension=0, tiled=True, axis_index_groups=rings(zs))
    return total[0].astype(f32)


def shards(tokens, segment_ids, cotangent, norm_gains, mixing, w_value, w_out, w_up, w_down):
    size = lax.axis_size("dp")
    zs = size // 4 if size == 16 else None
    is_enc = (lax.axis_index("section") == 0).astype(jnp.int32)
    core = lax.axis_index("dp").astype(jnp.int32) % 2
    flag = jnp.stack([is_enc, core])
    count = tokens.shape[0] // L
    rows = range(count)
    heads, width = mixing.shape[1], tokens.shape[1]
    seg = segment_ids.reshape(count, L)
    gains = norm_gains[0]
    args = (flag, seg, gains)
    weights = (mixing[0], w_value[0], w_out[0], w_up[0], w_down[0])
    sent = []
    for r in rows:
        if r == 0:
            y, weights = forward_row(r, *args, tokens, None, weights, first=True)
        else:
            y = forward_row(r, *args, tokens, None, weights)
        sent.append(lax.ppermute(y, "section", [(0, 1)]))
    ys, saved, back = [], [], []
    for r in rows:
        y, res = forward_row(r, *args, tokens, sent[r], weights)
        ys.append(y)
        saved.append(res)
        dx = backward_row(r, *args, cotangent, None, weights, res)
        back.append(lax.ppermute(dx, "section", [(1, 0)]))
    dxs, grads = [], []
    for r in rows:
        dx, got = backward_row(r, *args, cotangent, back[r], weights, saved[r])
        dxs.append(dx)
        grads.append(got)
    pick = lambda pieces, name: [p[name] for p in pieces]
    gain = sum(pick(grads, "dg"))
    per = width // size
    by_device = gain.reshape(2, size, per).transpose(1, 0, 2).reshape(size, 2 * per)
    by_device = jnp.pad(by_device, ((0, 0), (0, width - 2 * per)))
    down = down_grad(zs, flag, pick(grads, "dy"), pick(saved, "z"))
    up = up_grad(zs, flag, pick(grads, "du"), pick(saved, "a2"))
    mix = mix_grad(zs, flag, seg, weights[0], pick(grads, "don"), pick(saved, "o"), pick(saved, "v"))
    small = small_grad(
        zs, flag, by_device, pick(grads, "dml"), pick(saved, "o"), pick(grads, "dvt"), pick(saved, "a1")
    )
    if zs is None:
        scatter = lambda g, at: lax.psum_scatter(g, "dp", scatter_dimension=at, tiled=True)
        down_g = scatter(down[0], 0).T
        up_g = scatter(up[0], 0).T
        out_g = scatter(small[0], 0).T
        value_g = scatter(small[1], 0).T
        mix_g = scatter(mix[0], 1)
        gains_g = scatter(gain, 1)
    else:
        wide = ring_sum(jnp.concatenate([pair_sum(*down, size), pair_sum(*up, size)], axis=1), zs)
        rest = ring_sum(jnp.concatenate([pair_sum(*mix, size), pair_sum(*small, size)], axis=1), zs)
        ff = w_up.shape[2]
        cut = ff // size
        down_g = wide[:cut].reshape(ff // width, per, width).transpose(0, 2, 1).reshape(ff, per)
        up_g = wide[cut:].T
        query = L // size
        cut = heads * query * L // width
        strip = rest[:cut].reshape(heads // 3, 2, query, width)
        half = L // 2
        mix_g = jnp.stack(
            [
                strip[:, 0, :, :L],
                jnp.concatenate([strip[:, 0, :, L:], strip[:, 1, :, :half]], axis=-1),
                strip[:, 1, :, half:],
            ],
            axis=1,
        ).reshape(heads, query, L)
        out_g = rest[cut : cut + per].T
        value_g = rest[cut + per : cut + 2 * per].T
        gains_g = rest[cut + 2 * per, : 2 * per].reshape(2, per)
    return (
        jnp.concatenate(ys, axis=0)[None],
        jnp.concatenate(dxs, axis=0)[None],
        gains_g[None],
        mix_g[None],
        value_g[None],
        out_g[None],
        up_g[None],
        down_g[None],
    )


def solution(mesh):
    placed = (
        P("dp", None),
        P("dp"),
        P("dp", None),
        P("section", None, None),
        P("section", None, None, None),
        P("section", None, None),
        P("section", None, None),
        P("section", None, None),
        P("section", None, None),
    )
    return jax.shard_map(
        shards,
        mesh=mesh,
        in_specs=placed,
        out_specs=(
            P("section", "dp", None),
            P("section", "dp", None),
            P("section", None, "dp"),
            P("section", None, "dp", None),
            P("section", None, "dp"),
            P("section", None, "dp"),
            P("section", None, "dp"),
            P("section", None, "dp"),
        ),
        check_vma=False,
    )
```

```python
import functools
import jax
import jax.numpy as jnp
from jax import lax
from jax.experimental import pallas as pl
from jax.experimental.pallas import tpu as pltpu
from jax.sharding import PartitionSpec as P

L = 512
HD = 64
eps_norm = 1e-06
bf16 = jnp.bfloat16
f32 = jnp.float32
C0 = 0.7978845608028654
C1 = C0 * 0.044715
RC = 128
MIB = 1024 * 1024
ANY = pl.BlockSpec(memory_space=pl.ANY)
WHOLE = pl.BlockSpec(memory_space=pltpu.VMEM)
SMEM = pl.BlockSpec(memory_space=pltpu.SMEM)
sds = jax.ShapeDtypeStruct


def dot(a, b, ca, cb):
    return lax.dot_general(a, b, (((ca,), (cb,)), ((), ())), preferred_element_type=f32)


def rms_scale(values):
    return lax.rsqrt(jnp.mean(values * values, axis=-1, keepdims=True) + eps_norm)


def gelu_parts(u, want_slope):
    w = u * u
    h = 0.5 + 0.5 * jnp.tanh(u * (C0 + C1 * w))
    if not want_slope:
        return u * h, None
    slope = u * (C0 + (3.0 * C1) * w)
    return u * h, h + (h - h * h) * (slope + slope)


def build_mask(seg, is_enc, mask_ref):
    across = jnp.broadcast_to(seg, (128, L)).T
    for b in range(L // 128):
        same = across == seg[:, b * 128 : (b + 1) * 128]
        pos = lax.broadcasted_iota(jnp.int32, (L, 128), 0)
        key = lax.broadcasted_iota(jnp.int32, (L, 128), 1) + b * 128
        seen = (key <= pos) | (is_enc == 1)
        mask_ref[:, b * 128 : (b + 1) * 128] = jnp.where(same & seen, 1.0, 0.0).astype(bf16)


class Copies:
    def __init__(self, sems):
        self.sems = sems
        self.all = []

    def start(self, src, dst):
        copy = pltpu.make_async_copy(src, dst, self.sems.at[len(self.all)])
        copy.start()
        self.all.append(copy)
        return copy

    def wait(self):
        for copy in self.all:
            copy.wait()


RES = ("x", "a1", "v", "inv", "o", "m", "za", "g")


def hold(arrays):
    return [pltpu.with_memory_space_constraint(a, pltpu.VMEM) for a in arrays]


def far(arrays):
    return [pltpu.with_memory_space_constraint(a, pltpu.HBM) for a in arrays]


def mixed_far(pieces):
    return [p if i % 2 else far([p])[0] for i, p in enumerate(pieces)]


def attention_forward(gains, mask, xb, a1b, vb, ob, mb, invb, table, wv, wo, save, before_pair, before_out):
    for c in range(L // RC):
        rows = slice(c * RC, (c + 1) * RC)
        xf = xb[rows, :].astype(f32)
        a1b[rows, :] = (xf * rms_scale(xf) * gains[0:1, :]).astype(bf16)
    vb[...] = dot(a1b[...], wv[...], 1, 0).astype(bf16)
    save("a1", a1b)
    save("v", vb)
    low = lax.broadcasted_iota(jnp.int32, (L, 128), 1) < HD
    one = jnp.ones((L, 128), bf16)
    for p in range(table.shape[0] // 2):
        cols = slice(p * 128, (p + 1) * 128)
        before_pair(p)
        vp = vb[:, cols]
        even = dot(table[2 * p] * mask[...], jnp.where(low, vp, one), 1, 0)
        odd = dot(table[2 * p + 1] * mask[...], jnp.where(low, one, vp), 1, 0)
        inv = 1.0 / pltpu.roll(jnp.where(low, odd, even), HD, 1)
        ob[:, cols] = (jnp.where(low, even, odd) * inv).astype(bf16)
        if invb is not None:
            invb[:, cols] = inv
    save("o", ob)
    if invb is not None:
        save("inv", invb)
    before_out()
    mb[...] = xb[...].astype(f32) + dot(ob[...], wo[...], 1, 0)
    save("m", mb)


def ff_forward(gains, mb, a2b, zb, gb, yb, wu, wd, save):
    width, ff = mb.shape[1], wu.shape[1]
    nf = ff // width
    for c in range(L // RC):
        rows = slice(c * RC, (c + 1) * RC)
        m = mb[rows, :]
        a2b[rows, :] = (m * rms_scale(m) * gains[1:2, :]).astype(bf16)
    save("za", a2b, slice(None), pl.ds(ff, width))
    acc = mb[...]
    u = None
    for k in range(nf + 1):
        if k < nf:
            following = dot(a2b[...], wu[:, k * width : (k + 1) * width], 1, 0)
        if k > 0:
            cols = slice((k - 1) * width, k * width)
            z, g = gelu_parts(u, gb is not None)
            z = z.astype(bf16)
            if gb is not None:
                zb[:, cols] = z
                gb[:, cols] = g.astype(bf16)
                part = (slice(None), pl.ds((k - 1) * width, width))
                save("za", zb.at[part], *part)
                save("g", gb.at[part], *part)
            acc = acc + dot(z, wd[cols, :], 1, 0)
        u = following
    yb[...] = acc.astype(bf16)


def norm_back(grad, values, gain):
    scale = rms_scale(values)
    hat = values * scale
    scaled = grad * gain
    back = scale * (scaled - hat * jnp.mean(scaled * hat, axis=-1, keepdims=True))
    return back, jnp.sum(grad * hat, axis=0, keepdims=True)


def ff_backward(gains, dyb, gb, mb, accb, dmb, dmlb, put_du, wu, wd, before_slope, before_mid):
    width, ff = dyb.shape[1], wu.shape[1]
    nf = ff // width
    acc = None
    dz = None
    for k in range(nf + 1):
        if k < nf:
            following = dot(dyb[...], wd[k * width : (k + 1) * width, :], 1, 1)
        if k > 0:
            cols = slice((k - 1) * width, k * width)
            if k == 1:
                before_slope()
            part = (dz * gb[:, cols].astype(f32)).astype(bf16)
            put_du((k - 1) * width, part)
            more = dot(part, wu[:, cols], 1, 1)
            acc = more if acc is None else acc + more
        dz = following
    accb[...] = acc
    before_mid()
    dg = 0.0
    for c in range(L // RC):
        rows = slice(c * RC, (c + 1) * RC)
        back, add = norm_back(accb[rows, :], mb[rows, :], gains[1:2, :])
        dg = dg + add
        dm = dyb[rows, :].astype(f32) + back
        dmb[rows, :] = dm
        dmlb[rows, :] = dm.astype(bf16)
    return dg


def attention_backward(gains, mask, dmb, dmlb, invb, donb, dvtb, at, accb, xb, dxb, table, wv, wo, before_last):
    donb[at : at + L, :] = (dot(dmlb[...], wo[...], 1, 1) * invb[...]).astype(bf16)
    for p in range(table.shape[0] // 2):
        turned = donb[at : at + L, p * 128 : (p + 1) * 128].T
        for e in range(2):
            part = dot(turned[e * HD : (e + 1) * HD], table[2 * p + e] * mask[...], 1, 0)
            row = p * 128 + e * HD
            dvtb[row : row + HD, at : at + L] = part.astype(bf16)
    accb[...] = dot(dvtb[:, at : at + L], wv[...], 0, 1)
    before_last()
    dg = 0.0
    for c in range(L // RC):
        rows = slice(c * RC, (c + 1) * RC)
        back, add = norm_back(accb[rows, :], xb[rows, :].astype(f32), gains[0:1, :])
        dg = dg + add
        dxb[rows, :] = (dmb[rows, :] + back).astype(dxb.dtype)
    return dg


def params(limit, macs, name):
    return dict(
        compiler_params=pltpu.CompilerParams(vmem_limit_bytes=limit * MIB),
        cost_estimate=pl.CostEstimate(flops=2 * macs, bytes_accessed=20_000_000, transcendentals=0),
        name=name,
    )


def nothing(*unused):
    pass


def forward_kernel(first, row, *refs):
    it = iter(refs)
    take = lambda n: [next(it) for _ in range(n)]
    flag, seg, gains, tok = take(4)
    src = take(5)
    y_out = next(it)
    table, wv, wo, wu, wd = take(5) if first else src
    xb, mask, a1b, vb, ob, mb, a2b, yb, sin = take(9)
    width, ff = tok.shape[1], wu.shape[1]
    nf = ff // width
    ins = Copies(sin)
    cx = ins.start(tok.at[pl.ds(row * L, L)], xb)
    if first:
        cv = ins.start(src[1], wv)
        ct = [ins.start(src[0].at[pl.ds(2 * p, 2)], table.at[pl.ds(2 * p, 2)]) for p in range(table.shape[0] // 2)]
        co = ins.start(src[2], wo)
        cu = [ins.start(src[3], wu), ins.start(src[4], wd)]
    build_mask(seg[row : row + 1, :].astype(f32), flag[0], mask)
    cx.wait()

    def before_pair(p):
        if first:
            ct[p].wait()
            for h in (2 * p, 2 * p + 1):
                table[h] = jnp.exp(table[h].astype(f32)).astype(bf16)

    def before_out():
        if first:
            co.wait()
            for c in cu:
                c.wait()

    if first:
        cv.wait()
    attention_forward(gains, mask, xb, a1b, vb, ob, mb, None, table, wv, wo, nothing, before_pair, before_out)
    ff_forward(gains, mb, a2b, None, None, yb, wu, wd, nothing)
    done = ins.start(yb, y_out)
    done.wait()


def forward_row(row, flag, seg, gains, tok, weights, first=False):
    width, ff, heads = tok.shape[1], weights[3].shape[1], weights[0].shape[0]
    V = pltpu.VMEM
    out_shape, out_specs = [pltpu.HBM((L, width), bf16)], [ANY]
    if first:
        out_shape += [V(w.shape, w.dtype) for w in weights]
        out_specs += [WHOLE] * 5
    one = V((L, width), bf16)
    got = pl.pallas_call(
        functools.partial(forward_kernel, first, row),
        out_shape=out_shape,
        in_specs=[SMEM, WHOLE, WHOLE, ANY] + [ANY if first else WHOLE] * 5,
        out_specs=out_specs,
        scratch_shapes=[one, V((L, L), bf16), one, one, one, V((L, width), f32), one, one, pltpu.SemaphoreType.DMA((16,))],
        **params(20, L * width * (2 * width + 2 * ff) + 2 * heads * L * L * 128, "forward_first" if first else "forward"),
    )(flag, seg, gains, *far([tok]), *(far(weights) if first else hold(weights)))
    return (got[0], got[1:6]) if first else got[0]


def both_kernel(row, *refs):
    it = iter(refs)
    take = lambda n: [next(it) for _ in range(n)]
    flag, seg, gains, tok, recv, cot, table, wv, wo, wu, wd = take(11)
    y_out, dx_out = take(2)
    res = dict(zip(RES, take(len(RES))))
    xb, mask, a1b, vb, ob, mb, a2b, yb, rb, invb, zb, gb = take(12)
    dyb, accb, dmb, dmlb, donb, dvtb, dxb, sin, sout = take(9)
    ins, outs = Copies(sin), Copies(sout)

    def save(name, src_ref, *where):
        dst = res[name]
        outs.start(src_ref, dst.at[where] if where else dst)

    cr = ins.start(recv, rb)
    cx = ins.start(tok.at[pl.ds(row * L, L)], xb)
    cy = ins.start(cot.at[pl.ds(row * L, L)], dyb)
    is_enc = flag[0]
    build_mask(seg[row : row + 1, :].astype(f32), is_enc, mask)
    cx.wait()
    cr.wait()
    xb[...] = jnp.where(is_enc == 1, xb[...], rb[...])
    save("x", xb)
    attention_forward(gains, mask, xb, a1b, vb, ob, mb, invb, table, wv, wo, save, nothing, nothing)
    ff_forward(gains, mb, a2b, zb, gb, yb, wu, wd, save)
    outs.start(yb, y_out)
    cy.wait()
    ff_backward(gains, dyb, gb, mb, accb, dmb, dmlb, nothing, wu, wd, nothing, nothing)
    attention_backward(gains, mask, dmb, dmlb, invb, donb, dvtb, 0, accb, xb, dxb, table, wv, wo, nothing)
    outs.start(dxb, dx_out)
    outs.wait()


def both_row(row, flag, seg, gains, tok, recv, cot, weights):
    width, ff, heads = tok.shape[1], weights[3].shape[1], weights[0].shape[0]
    V = pltpu.VMEM
    wide = lambda dt: pltpu.HBM((L, width), dt)
    out_shape = [wide(bf16)] * 5 + [wide(f32), wide(bf16), wide(f32)]
    out_shape += [pltpu.HBM((L, ff + width), bf16), pltpu.HBM((L, ff), bf16)]
    one = V((L, width), bf16)
    big = V((L, width), f32)
    full = V((L, ff), bf16)
    got = pl.pallas_call(
        functools.partial(both_kernel, row),
        out_shape=out_shape,
        in_specs=[SMEM, WHOLE, WHOLE] + [ANY] * 3 + [WHOLE] * 5,
        out_specs=[ANY] * len(out_shape),
        scratch_shapes=[one, V((L, L), bf16), one, one, one, big, one, one, one, big, full, full]
        + [one, big, big, one, one, V((width, L), bf16), one]
        + [pltpu.SemaphoreType.DMA((4,)), pltpu.SemaphoreType.DMA((20,))],
        **params(32, 2 * L * width * (2 * width + 2 * ff) + 3 * heads * L * L * 128, "forward_backward"),
    )(flag, seg, gains, *far([tok]), recv, *far([cot]), *hold(weights))
    return got[0], got[1], dict(zip(RES, got[2:]))


def ring_place(zy, zs):
    z, y = zy // 2, zy % 2
    return z if y == 0 else 2 * zs - 1 - z


def put_halves(core, block, keep, send, at):
    half = block.shape[0] // 2
    top, bottom = block[:half], block[half:]
    keep[at] = jnp.where(core == 0, top, bottom).astype(keep.dtype)
    send[at] = jnp.where(core == 0, bottom, top).astype(send.dtype)


def turn_into(zs, core, width, ff, turned):
    def put(first, part):
        t = part.T
        if zs is None:
            turned[0][first : first + t.shape[0], :] = t
            return
        pair = (ff if first < ff else width) // (2 * zs)
        base = 0 if first < ff else ff // 2
        for s in range(t.shape[0] // pair):
            place = ring_place((first - 2 * base) // pair + s, zs)
            row = base + place * (pair // 2)
            put_halves(core, t[s * pair : (s + 1) * pair], turned[0], turned[1], slice(row, row + pair // 2))

    return put


def backward_kernel(zs, row, part, *refs):
    it = iter(refs)
    take = lambda n: [next(it) for _ in range(n)]
    n_turn = 1 if zs is None else 2
    flag, gains, cot, recv, wu, wd, m, g = take(8)
    if part == 0:
        seg, table, wv, wo, x, inv = take(6)
    turned_out = take(n_turn)
    dml_out, dm_out, dg_out = take(3)
    if part == 0:
        don_out, dvt_out = take(2)
    turned = take(n_turn)
    dyb, gb, mb, accb, dmlb, rb = take(6)
    if part == 0:
        mask, invb, xb, donb, dvtb = take(5)
    sin, sout = take(2)
    width, ff = dyb.shape[1], gb.shape[1]
    is_enc = flag[0]
    ins, outs = Copies(sin), Copies(sout)
    cy = ins.start(cot.at[pl.ds(row * L, L)], dyb)
    cr = ins.start(recv, rb)
    cg, cm = ins.start(g, gb), ins.start(m, mb)
    if part == 0:
        ci, cx = ins.start(inv, invb), ins.start(x, xb)
        build_mask(seg[row : row + 1, :].astype(f32), is_enc, mask)
    cy.wait()
    cr.wait()
    dyb[...] = jnp.where(is_enc == 1, rb[...], dyb[...])
    put = turn_into(zs, flag[1], width, ff, turned)
    put(ff, dyb[...])
    dg2 = ff_backward(gains, dyb, gb, mb, accb, mb, dmlb, put, wu, wd, cg.wait, cm.wait)
    for src, dst in zip(turned, turned_out):
        outs.start(src, dst)
    outs.start(dmlb, dml_out)
    dg1 = jnp.zeros_like(dg2)
    if part == 0:
        ci.wait()
        cx.wait()
        dg1 = attention_backward(gains, mask, mb, dmlb, invb, donb, dvtb, 0, accb, xb, mb, table, wv, wo, nothing)
        outs.start(donb, don_out)
        outs.start(dvtb, dvt_out)
    outs.start(mb, dm_out)
    dg_out[0:1, :] = dg1
    dg_out[1:2, :] = dg2
    outs.wait()


def backward_row(zs, row, flag, seg, gains, cot, recv, weights, res, part):
    width, ff, heads = cot.shape[1], weights[3].shape[1], weights[0].shape[0]
    V = pltpu.VMEM
    wide = lambda dt: pltpu.HBM((L, width), dt)
    tall = (ff + width if zs is None else (ff + width) // 2, L)
    n_turn = 1 if zs is None else 2
    one, big, full = V((L, width), bf16), V((L, width), f32), V((L, ff), bf16)
    out_shape = [pltpu.HBM(tall, bf16)] * n_turn + [wide(bf16), wide(f32), sds((2, width), f32)]
    out_specs = [ANY] * (n_turn + 2) + [WHOLE]
    scratch = [V(tall, bf16)] * n_turn + [one, full, big, big, one, one]
    ins = [flag, gains, *far([cot]), recv, *hold(weights[3:]), *far([res["m"], res["g"]])]
    specs = [SMEM, WHOLE, ANY, ANY, WHOLE, WHOLE, ANY, ANY]
    names = ["send"][: n_turn - 1] + ["dml", "dm", "dg"]
    if part == 0:
        out_shape += [wide(bf16), pltpu.HBM((width, L), bf16)]
        out_specs += [ANY, ANY]
        names += ["don", "dvt"]
        scratch += [V((L, L), bf16), big, one, one, V((width, L), bf16)]
        ins += [seg, *hold(weights[:3]), *far([res["x"], res["inv"]])]
        specs += [WHOLE] * 4 + [ANY, ANY]
    macs = 2 * L * width * ff + (0 if part else 2 * L * width * width + 2 * heads * L * L * 64)
    got = pl.pallas_call(
        functools.partial(backward_kernel, zs, row, part),
        out_shape=out_shape,
        in_specs=specs,
        out_specs=out_specs,
        scratch_shapes=scratch + [pltpu.SemaphoreType.DMA((8,)), pltpu.SemaphoreType.DMA((8,))],
        **params(32 if part == 0 else 26, macs, "ff_backward" if part else "backward"),
    )(*ins)
    return dict(zip(["own"] + names, got))


def wide_kernel(zs, count, which, *refs):
    turned, za = refs[:count], refs[count : 2 * count]
    out, left, right, stage, sin, sout = refs[-6:]
    ins, outs = Copies(sin), Copies(sout)
    n_left, depth = left.shape
    n_right = right.shape[1]
    top = 0 if which else turned[0].shape[0] - n_left
    step = n_right if which else stage.shape[-1]
    ff = za[0].shape[1] - n_right
    lanes = lambda k: pl.ds(ff, n_right) if which else pl.ds(k * step, step)
    first = [ins.start(t.at[pl.ds(top, n_left)], left.at[:, pl.ds(r * L, L)]) for r, t in enumerate(turned)]
    waits = []
    for k in range(n_right // step):
        put = pl.ds(k * step, step)
        waits.append([ins.start(a.at[:, lanes(k)], right.at[pl.ds(r * L, L), put]) for r, a in enumerate(za)])
    for c in first:
        c.wait()
    if which:
        for c in waits[0]:
            c.wait()
        some = n_left // 2
        for i in range(2):
            got = dot(left[i * some : (i + 1) * some, :], right[...], 1, 0).astype(bf16)
            if zs is None:
                at = pl.ds(i * some, some)
                stage[at] = got
                outs.start(stage.at[at], out.at[at])
            else:
                at = pl.ds(i * zs, zs)
                stage[at] = got.reshape(zs, some // zs, step)
                outs.start(stage.at[at], out.at[at, pl.ds(out.shape[1] // 2, some // zs)])
    else:
        for k in range(n_right // step):
            for c in waits[k]:
                c.wait()
            got = dot(left[...], right[:, k * step : (k + 1) * step], 1, 0).astype(bf16)
            if zs is None:
                at = (slice(None), pl.ds(k * step, step))
                stage[:, k * step : (k + 1) * step] = got
                outs.start(stage.at[at], out.at[at])
            else:
                per = n_left // (2 * zs)
                at = (slice(None), pl.ds(k * per, per))
                stage[:, k * per : (k + 1) * per, :] = got.reshape(2 * zs, per, step)
                outs.start(stage.at[at], out.at[at])
    outs.wait()


def wide_grad(zs, width, which, turned, za, before=None):
    count = len(turned)
    depth = count * L
    ff = za[0].shape[1] - width
    halves = 1 if zs is None else 2
    n_left, n_right = (ff // halves, width) if which else (width // halves, ff)
    V = pltpu.VMEM
    if zs is None:
        out = pltpu.HBM((ff, width) if which else (width, ff), bf16)
        stage = V((n_left, n_right), bf16)
    else:
        out = pltpu.HBM((2 * zs, ff // (2 * zs), width), bf16)
        stage = V((2 * zs, ff // (4 * zs), width), bf16)
    ins = [*mixed_far(turned), *mixed_far(za)] + ([] if before is None else far([before]))
    return pl.pallas_call(
        functools.partial(wide_kernel, zs, count, which),
        out_shape=out,
        in_specs=[ANY] * len(ins),
        out_specs=ANY,
        input_output_aliases={} if before is None else {len(ins) - 1: 0},
        scratch_shapes=[V((n_left, depth), bf16), V((depth, n_right), bf16), stage]
        + [pltpu.SemaphoreType.DMA((5 * count,)), pltpu.SemaphoreType.DMA((4,))],
        **params(24, depth * n_left * n_right, "up_grad" if which else "down_grad"),
    )(*ins)


def rest_kernel(zs, *refs):
    it = iter(refs)
    take = lambda n: [next(it) for _ in range(n)]
    flag, seg, gains, table, wv, wo = take(6)
    dm, dml_last, dg2, inv, x, o_last, v_last, a1_last = take(8)
    rows = (len(refs) - 6 - 8 - (4 if zs is None else 3) - 13) // 7
    dml, don, dvt, dg, o, v, a1 = [take(rows) for _ in range(7)]
    outs_w = take(3 if zs is None else 2)
    dx_out = next(it)
    if zs is None:
        gain_out = outs_w[2]
    mask, dmb, dmlb, invb, xb, accb, donb, dvtb, ob, vb, a1b, gainb, sin = take(13)
    is_enc, core = flag[0], flag[1]
    heads, width = table.shape[0], ob.shape[1]
    last = rows * L
    ins = Copies(sin)
    dml_at = lambda r: dmlb.at[pl.ds(r * L, L)]
    early = [ins.start(dml_last, dml_at(rows)), ins.start(inv, invb)]
    mid = [ins.start(dm, dmb), ins.start(x, xb)]
    ready = [ins.start(v_last, vb.at[pl.ds(last, L)]), ins.start(o_last, ob.at[pl.ds(last, L)])]
    for r in range(rows):
        at = pl.ds(r * L, L)
        ready += [ins.start(v[r], vb.at[at]), ins.start(o[r], ob.at[at]), ins.start(don[r], donb.at[at])]
    later = [ins.start(a1_last, a1b.at[pl.ds(last, L)])]
    for r in range(rows):
        at = pl.ds(r * L, L)
        later += [ins.start(dml[r], dmlb.at[at]), ins.start(a1[r], a1b.at[at]), ins.start(dvt[r], dvtb.at[:, at])]
    for r in range(rows + 1):
        build_mask(seg[r : r + 1, :].astype(f32), is_enc, mask.at[r])
    for c in early:
        c.wait()
    mine = mask.at[rows]

    def before_last():
        for c in mid:
            c.wait()

    dg1 = attention_backward(
        gains, mine, dmb, dmlb.at[pl.ds(last, L)], invb, donb, dvtb, last, accb, xb, dmb, table, wv, wo, before_last
    )
    sent = ins.start(dmb, dx_out)
    gainb[...] = jnp.zeros_like(gainb)
    gainb[0:2, :] = dg2[...]
    gainb[0:1, :] = dg1
    for r in range(rows):
        gainb[0:2, :] += dg[r][...]
    for c in ready:
        c.wait()
    lane = lax.broadcasted_iota(jnp.int32, (L, 128), 1)
    low = lane < HD
    one = jnp.ones((L, 128), bf16)
    for p in range(heads // 2):
        cols = slice(p * 128, (p + 1) * 128)
        total = [0.0, 0.0]
        for r in range(rows + 1):
            at = slice(r * L, (r + 1) * L)
            dn, vp = donb[at, cols], vb[at, cols]
            prod = dn.astype(f32) * ob[at, cols].astype(f32)
            for e in range(2):
                own = low if e == 0 else ~low
                delta = jnp.sum(jnp.where(own, prod, 0.0), axis=-1, keepdims=True) * (-1.0 / 32.0)
                high = delta.astype(bf16)
                less = (delta - high.astype(f32)).astype(bf16)
                fill = jnp.where((lane & (HD - 1)) < 32, high, less)
                term = dot(jnp.where(own, dn, fill), jnp.where(own, vp, one), 1, 1) * mask[r].astype(f32)
                total[e] = term if r == 0 else total[e] + term
        for e in range(2):
            h = 2 * p + e
            ds = total[e] * table[h].astype(f32)
            if zs is None:
                outs_w[0][h] = ds
                continue
            per = L // (4 * zs)
            cut = width - L
            pieces = [[(0, 0, 0, L)], [(0, L, 0, cut), (1, 0, cut, L)], [(1, L - cut, 0, L)]][h % 3]
            for s in range(2 * zs):
                block = ds[2 * per * s : 2 * per * (s + 1)]
                for strip, lane_at, a, b in pieces:
                    row_at = ((h // 3) * 2 + strip) * per
                    at = (ring_place(s, zs), slice(row_at, row_at + per), slice(lane_at, lane_at + b - a))
                    put_halves(core, block[:, a:b], outs_w[0], outs_w[1], at)
    for c in later:
        c.wait()
    for i in range(2):
        got = dot(dmlb[...], ob[...], 0, 0) if i == 0 else dot(dvtb[...], a1b[...], 1, 0)
        if zs is None:
            outs_w[1][i] = got.astype(bf16)
            continue
        per = width // (4 * zs)
        base = heads * L * L // (4 * zs * width)
        for s in range(2 * zs):
            at = (ring_place(s, zs), slice(base + i * per, base + (i + 1) * per))
            put_halves(core, got[2 * per * s : 2 * per * (s + 1)], outs_w[0], outs_w[1], at)
    if zs is None:
        gain_out[...] = gainb[0:2, :]
    else:
        for s in range(2 * zs):
            turns = [gainb[...] if d == 0 else pltpu.roll(gainb[...], width - d * per, 1) for d in (2 * s, 2 * s + 1)]
            at = (ring_place(s, zs), slice(base + 2 * per, base + 2 * per + 16))
            put_halves(core, jnp.concatenate(turns, axis=0), outs_w[0], outs_w[1], at)
    sent.wait()


def rest_grads(zs, flag, seg, gains, weights, saved, grads, mid):
    width, heads = saved[0]["x"].shape[1], weights[0].shape[0]
    rows, last = len(grads), saved[-1]
    V = pltpu.VMEM
    one, big = V((L, width), bf16), V((L, width), f32)
    tall = V(((rows + 1) * L, width), bf16)
    if zs is None:
        blocks = [sds((heads, L, L), f32), sds((2, width, width), bf16), sds((2, width), f32)]
    else:
        size = 4 * zs
        blocks = [sds((2 * zs, heads * L * L // (size * width) + 2 * width // size + 16, width), bf16)] * 2
    front = far([mid["dm"], mid["dml"]]) + [mid["dg"]] + far([last[n] for n in ("inv", "x", "o", "v", "a1")])
    old = saved[:-1]
    back = far(pick(grads, "dml") + pick(grads, "don") + pick(grads, "dvt")) + pick(grads, "dg")
    back += far(pick(old, "o") + pick(old, "v") + pick(old, "a1"))
    specs = [SMEM] + [WHOLE] * 5 + [ANY, ANY, WHOLE] + [ANY] * 5 + [ANY] * (3 * rows) + [WHOLE] * rows + [ANY] * (3 * rows)
    got = pl.pallas_call(
        functools.partial(rest_kernel, zs),
        out_shape=blocks + [pltpu.HBM((L, width), f32)],
        in_specs=specs,
        out_specs=[WHOLE] * len(blocks) + [ANY],
        scratch_shapes=[V((rows + 1, L, L), bf16), big, tall, big, one, big, tall, V((width, (rows + 1) * L), bf16), tall, tall, tall]
        + [V((16, width), f32), pltpu.SemaphoreType.DMA((10 + 6 * rows,))],
        **params(40, (rows + 3) * 2 * L * width * width + (rows + 2) * heads * L * L * 128, "rest_grads"),
    )(flag, seg, gains, *hold(weights[:3]), *front, *back)
    return got[:-1], got[-1]


def unpack_kernel(per, rest, mix_out, value_out, out_out, gain_out):
    heads, query, _ = mix_out.shape
    width = rest.shape[1]
    cut = width - L
    for h in range(heads):
        at = (h // 3) * 2 * query
        first, second = slice(at, at + query), slice(at + query, at + 2 * query)
        if h % 3 == 0:
            mix_out[h] = rest[first, 0:L].astype(f32)
        elif h % 3 == 1:
            mix_out[h, :, 0:cut] = rest[first, L:].astype(f32)
            mix_out[h, :, cut:] = rest[second, 0 : L - cut].astype(f32)
        else:
            mix_out[h] = rest[second, L - cut :].astype(f32)
    base = heads * query * L // width
    out_out[...] = rest[base : base + per, :].astype(f32).T
    value_out[...] = rest[base + per : base + 2 * per, :].astype(f32).T
    gain_out[...] = rest[base + 2 * per : base + 2 * per + 16, :].astype(f32)[0:2, 0:per]


def unpack(rest, heads, per, query):
    width = rest.shape[1]
    shapes = [(heads, query, L), (width, per), (width, per), (2, per)]
    return pl.pallas_call(
        functools.partial(unpack_kernel, per),
        out_shape=[sds(s, f32) for s in shapes],
        in_specs=[WHOLE],
        out_specs=[WHOLE] * 4,
        **params(12, 1000, "unpack"),
    )(rest)


def pick(pieces, name):
    return [p[name] for p in pieces]


def rings(zs):
    order = sorted(range(2 * zs), key=lambda s: ring_place(s, zs))
    return [[2 * s + c for s in order] for c in range(2)]


def ring_sum(blocks, size):
    return lax.psum_scatter(blocks, "dp", scatter_dimension=0, tiled=True, axis_index_groups=rings(size // 4))[0]


def shards(tokens, segment_ids, cotangent, norm_gains, mixing, w_value, w_out, w_up, w_down):
    size = lax.axis_size("dp")
    zs = size // 4 if size == 16 else None
    is_enc = (lax.axis_index("section") == 0).astype(jnp.int32)
    core = lax.axis_index("dp").astype(jnp.int32) % 2
    flag = jnp.stack([is_enc, core])
    count = tokens.shape[0] // L
    heads, width, ff = mixing.shape[1], tokens.shape[1], w_up.shape[2]
    seg = segment_ids.reshape(count, L)
    gains = norm_gains[0]
    args = (flag, seg, gains)
    weights = (mixing[0], w_value[0], w_out[0], w_up[0], w_down[0])
    sent, ys, saved, back, dxs, grads = [], [], [], [], [], []
    for r in range(count):
        if r == 0:
            y, weights = forward_row(r, *args, tokens, weights, first=True)
        else:
            y = forward_row(r, *args, tokens, weights)
        sent.append(lax.ppermute(y, "section", [(0, 1)]))
    for r in range(count):
        y, dx, res = both_row(r, *args, tokens, sent[r], cotangent, weights)
        ys.append(y)
        saved.append(res)
        back.append(lax.ppermute(dx, "section", [(1, 0)]))
    swap = lambda a: lax.ppermute(a, "dp", [(d, d ^ 1) for d in range(size)])
    turned = []
    za = pick(saved, "za")
    if zs is not None:
        *za, back[0] = lax.optimization_barrier((*za, back[0]))
    for r in range(count):
        got = backward_row(zs, r, *args, cotangent, back[r], weights, saved[r], int(r == count - 1))
        turned.append(got["own"])
        if r < count - 1:
            dxs.append(got["dm"])
            grads.append(got)
        if zs is not None:
            turned.append(swap(got["send"]))
            za.insert(2 * r + 1, swap(za[2 * r]))
    if zs is None:
        wide = [wide_grad(zs, width, w, turned, za) for w in (0, 1)]
        held = saved
    else:
        wide = wide_grad(zs, width, 1, turned, za, wide_grad(zs, width, 0, turned, za))
        held, wide = lax.optimization_barrier((saved, wide))
    rest, dx = rest_grads(zs, *args, weights, held, grads, got)
    dxs.append(dx)
    per = width // size
    if zs is None:
        scatter = lambda g, at: lax.psum_scatter(g.astype(f32), "dp", scatter_dimension=at, tiled=True)
        down_g = scatter(wide[0], 0).T
        up_g = scatter(wide[1], 0).T
        out_g = scatter(rest[1][0], 0).T
        value_g = scatter(rest[1][1], 0).T
        mix_g = scatter(rest[0], 1)
        gains_g = scatter(rest[2], 1)
    else:
        wide = ring_sum(wide, size)
        cut = ff // size
        down_g = wide[:cut].reshape(ff // width, per, width).transpose(0, 2, 1).reshape(ff, per).astype(f32)
        up_g = wide[cut:].T.astype(f32)
        mix_g, value_g, out_g, gains_g = unpack(ring_sum(rest[0] + swap(rest[1]), size), heads, per, L // size)
    return (
        jnp.concatenate(ys, axis=0)[None],
        jnp.concatenate(dxs, axis=0)[None],
        gains_g[None],
        mix_g[None],
        value_g[None],
        out_g[None],
        up_g[None],
        down_g[None],
    )


def solution(mesh):
    placed = (
        P("dp", None),
        P("dp"),
        P("dp", None),
        P("section", None, None),
        P("section", None, None, None),
        P("section", None, None),
        P("section", None, None),
        P("section", None, None),
        P("section", None, None),
    )
    return jax.shard_map(
        shards,
        mesh=mesh,
        in_specs=placed,
        out_specs=(
            P("section", "dp", None),
            P("section", "dp", None),
            P("section", None, "dp"),
            P("section", None, "dp", None),
            P("section", None, "dp"),
            P("section", None, "dp"),
            P("section", None, "dp"),
            P("section", None, "dp"),
        ),
        check_vma=False,
    )
```

```python
import functools
import jax
import jax.numpy as jnp
from jax import lax
from jax.experimental import pallas as pl
from jax.experimental.pallas import tpu as pltpu
from jax.sharding import PartitionSpec as P

L = 512
HD = 64
eps_norm = 1e-06
bf16 = jnp.bfloat16
f32 = jnp.float32
C0 = 0.7978845608028654
C1 = C0 * 0.044715
RC = 128
MIB = 1024 * 1024
ANY = pl.BlockSpec(memory_space=pl.ANY)
WHOLE = pl.BlockSpec(memory_space=pltpu.VMEM)
SMEM = pl.BlockSpec(memory_space=pltpu.SMEM)
sds = jax.ShapeDtypeStruct


def dot(a, b, ca, cb):
    return lax.dot_general(a, b, (((ca,), (cb,)), ((), ())), preferred_element_type=f32)


def rms_scale(values):
    return lax.rsqrt(jnp.mean(values * values, axis=-1, keepdims=True) + eps_norm)


def gelu_parts(u, want_slope):
    w = u * u
    h = 0.5 + 0.5 * jnp.tanh(u * (C0 + C1 * w))
    if not want_slope:
        return u * h, None
    slope = u * (C0 + (3.0 * C1) * w)
    return u * h, h + (h - h * h) * (slope + slope)


def build_mask(seg, is_enc, mask_ref):
    across = jnp.broadcast_to(seg, (128, L)).T
    for b in range(L // 128):
        same = across == seg[:, b * 128 : (b + 1) * 128]
        pos = lax.broadcasted_iota(jnp.int32, (L, 128), 0)
        key = lax.broadcasted_iota(jnp.int32, (L, 128), 1) + b * 128
        seen = (key <= pos) | (is_enc == 1)
        mask_ref[:, b * 128 : (b + 1) * 128] = jnp.where(same & seen, 1.0, 0.0).astype(bf16)


class Copies:
    def __init__(self, sems):
        self.sems = sems
        self.all = []

    def start(self, src, dst):
        copy = pltpu.make_async_copy(src, dst, self.sems.at[len(self.all)])
        copy.start()
        self.all.append(copy)
        return copy

    def wait(self):
        for copy in self.all:
            copy.wait()


RES = ("x", "a1", "v", "inv", "o", "m", "z", "a2", "g")


def hold(arrays):
    return [pltpu.with_memory_space_constraint(a, pltpu.VMEM) for a in arrays]


def far(arrays):
    return [pltpu.with_memory_space_constraint(a, pltpu.HBM) for a in arrays]


def mixed_far(pieces):
    return [p if i % 2 else far([p])[0] for i, p in enumerate(pieces)]


def attention_forward(gains, mask, xb, a1b, vb, ob, mb, invb, table, wv, wo, save, before_pair, before_out):
    for c in range(L // RC):
        rows = slice(c * RC, (c + 1) * RC)
        xf = xb[rows, :].astype(f32)
        a1b[rows, :] = (xf * rms_scale(xf) * gains[0:1, :]).astype(bf16)
    vb[...] = dot(a1b[...], wv[...], 1, 0).astype(bf16)
    save("a1", a1b)
    save("v", vb)
    low = lax.broadcasted_iota(jnp.int32, (L, 128), 1) < HD
    one = jnp.ones((L, 128), bf16)
    for p in range(table.shape[0] // 2):
        cols = slice(p * 128, (p + 1) * 128)
        before_pair(p)
        vp = vb[:, cols]
        even = dot(table[2 * p] * mask[...], jnp.where(low, vp, one), 1, 0)
        odd = dot(table[2 * p + 1] * mask[...], jnp.where(low, one, vp), 1, 0)
        inv = 1.0 / pltpu.roll(jnp.where(low, odd, even), HD, 1)
        ob[:, cols] = (jnp.where(low, even, odd) * inv).astype(bf16)
        if invb is not None:
            invb[:, cols] = inv
    save("o", ob)
    if invb is not None:
        save("inv", invb)
    before_out()
    mb[...] = xb[...].astype(f32) + dot(ob[...], wo[...], 1, 0)
    save("m", mb)


def ff_forward(gains, mb, a2b, zb, gb, yb, wu, wd, save):
    width, ff = mb.shape[1], wu.shape[1]
    nf = ff // width
    for c in range(L // RC):
        rows = slice(c * RC, (c + 1) * RC)
        m = mb[rows, :]
        a2b[rows, :] = (m * rms_scale(m) * gains[1:2, :]).astype(bf16)
    save("a2", a2b)
    acc = mb[...]
    u = None
    for k in range(nf + 1):
        if k < nf:
            following = dot(a2b[...], wu[:, k * width : (k + 1) * width], 1, 0)
        if k > 0:
            cols = slice((k - 1) * width, k * width)
            z, g = gelu_parts(u, gb is not None)
            z = z.astype(bf16)
            if gb is not None:
                zb[:, cols] = z
                gb[:, cols] = g.astype(bf16)
                part = (slice(None), pl.ds((k - 1) * width, width))
                save("z", zb.at[part], *part)
                save("g", gb.at[part], *part)
            acc = acc + dot(z, wd[cols, :], 1, 0)
        u = following
    yb[...] = acc.astype(bf16)


def norm_back(grad, values, gain):
    scale = rms_scale(values)
    hat = values * scale
    scaled = grad * gain
    back = scale * (scaled - hat * jnp.mean(scaled * hat, axis=-1, keepdims=True))
    return back, jnp.sum(grad * hat, axis=0, keepdims=True)


def ff_backward(gains, dyb, gb, mb, accb, dmb, dmlb, put_du, wu, wd, before_slope, before_mid):
    width, ff = dyb.shape[1], wu.shape[1]
    nf = ff // width
    acc = None
    dz = None
    for k in range(nf + 1):
        if k < nf:
            following = dot(dyb[...], wd[k * width : (k + 1) * width, :], 1, 1)
        if k > 0:
            cols = slice((k - 1) * width, k * width)
            if k == 1:
                before_slope()
            part = (dz * gb[:, cols].astype(f32)).astype(bf16)
            put_du((k - 1) * width, part)
            more = dot(part, wu[:, cols], 1, 1)
            acc = more if acc is None else acc + more
        dz = following
    accb[...] = acc
    before_mid()
    dg = 0.0
    for c in range(L // RC):
        rows = slice(c * RC, (c + 1) * RC)
        back, add = norm_back(accb[rows, :], mb[rows, :], gains[1:2, :])
        dg = dg + add
        dm = dyb[rows, :].astype(f32) + back
        dmb[rows, :] = dm
        dmlb[rows, :] = dm.astype(bf16)
    return dg


def attention_backward(gains, mask, dmb, dmlb, invb, donb, dvtb, at, accb, xb, dxb, table, wv, wo, before_last):
    donb[at : at + L, :] = (dot(dmlb[...], wo[...], 1, 1) * invb[...]).astype(bf16)
    for p in range(table.shape[0] // 2):
        turned = donb[at : at + L, p * 128 : (p + 1) * 128].T
        for e in range(2):
            part = dot(turned[e * HD : (e + 1) * HD], table[2 * p + e] * mask[...], 1, 0)
            row = p * 128 + e * HD
            dvtb[row : row + HD, at : at + L] = part.astype(bf16)
    accb[...] = dot(dvtb[:, at : at + L], wv[...], 0, 1)
    before_last()
    dg = 0.0
    for c in range(L // RC):
        rows = slice(c * RC, (c + 1) * RC)
        back, add = norm_back(accb[rows, :], xb[rows, :].astype(f32), gains[0:1, :])
        dg = dg + add
        dxb[rows, :] = (dmb[rows, :] + back).astype(dxb.dtype)
    return dg


def params(limit, macs, name):
    return dict(
        compiler_params=pltpu.CompilerParams(vmem_limit_bytes=limit * MIB),
        cost_estimate=pl.CostEstimate(flops=10 * macs, bytes_accessed=20_000_000, transcendentals=0),
        name=name,
    )


def nothing(*unused):
    pass


def forward_kernel(first, row, *refs):
    it = iter(refs)
    take = lambda n: [next(it) for _ in range(n)]
    flag, seg, gains, tok = take(4)
    src = take(5)
    y_out = next(it)
    table, wv, wo, wu, wd = take(5) if first else src
    xb, mask, a1b, vb, ob, mb, a2b, sin = take(8)
    width, ff = tok.shape[1], wu.shape[1]
    nf = ff // width
    ins = Copies(sin)
    cx = ins.start(tok.at[pl.ds(row * L, L)], xb)
    if first:
        cv = ins.start(src[1], wv)
        ct = [ins.start(src[0].at[pl.ds(2 * p, 2)], table.at[pl.ds(2 * p, 2)]) for p in range(table.shape[0] // 2)]
        co = ins.start(src[2], wo)
        cu = [ins.start(src[3], wu), ins.start(src[4], wd)]
    build_mask(seg[row : row + 1, :].astype(f32), flag[0], mask)
    cx.wait()

    def before_pair(p):
        if first:
            ct[p].wait()
            for h in (2 * p, 2 * p + 1):
                table[h] = jnp.exp(table[h].astype(f32)).astype(bf16)

    def before_out():
        if first:
            co.wait()
            for c in cu:
                c.wait()

    if first:
        cv.wait()
    attention_forward(gains, mask, xb, a1b, vb, ob, mb, None, table, wv, wo, nothing, before_pair, before_out)
    ff_forward(gains, mb, a2b, None, None, y_out, wu, wd, nothing)


def forward_row(row, flag, seg, gains, tok, weights, first=False):
    width, ff, heads = tok.shape[1], weights[3].shape[1], weights[0].shape[0]
    V = pltpu.VMEM
    out_shape, out_specs = [V((L, width), bf16)], [WHOLE]
    if first:
        out_shape += [V(w.shape, w.dtype) for w in weights]
        out_specs += [WHOLE] * 5
    one = V((L, width), bf16)
    got = pl.pallas_call(
        functools.partial(forward_kernel, first, row),
        out_shape=out_shape,
        in_specs=[SMEM, WHOLE, WHOLE, ANY] + [ANY if first else WHOLE] * 5,
        out_specs=out_specs,
        scratch_shapes=[one, V((L, L), bf16), one, one, one, V((L, width), f32), one, pltpu.SemaphoreType.DMA((16,))],
        **params(9, L * width * (2 * width + 2 * ff) + 2 * heads * L * L * 128, "forward_first" if first else "forward"),
    )(flag, seg, gains, *far([tok]), *(far(weights) if first else hold(weights)))
    return (got[0], got[1:6]) if first else got[0]


def both_kernel(row, *refs):
    it = iter(refs)
    take = lambda n: [next(it) for _ in range(n)]
    flag, seg, gains, tok, recv, cot, table, wv, wo, wu, wd = take(11)
    y_out, dx_out = take(2)
    res = dict(zip(RES, take(len(RES))))
    xb, mask, a1b, vb, ob, a2b, yb, rb, invb, zb = take(10)
    mb, gb = take(2)
    dyb, accb, dmb, dmlb, donb, dvtb, sin, sout = take(8)
    ins, outs = Copies(sin), Copies(sout)

    def save(name, src_ref, *where):
        dst = res[name]
        outs.start(src_ref, dst.at[where] if where else dst)

    cr = ins.start(recv, rb)
    cx = ins.start(tok.at[pl.ds(row * L, L)], xb)
    cy = ins.start(cot.at[pl.ds(row * L, L)], dyb)
    is_enc = flag[0]
    build_mask(seg[row : row + 1, :].astype(f32), is_enc, mask)
    cx.wait()
    cr.wait()
    xb[...] = jnp.where(is_enc == 1, xb[...], rb[...])
    save("x", xb)
    attention_forward(gains, mask, xb, a1b, vb, ob, mb, invb, table, wv, wo, save, nothing, nothing)
    ff_forward(gains, mb, a2b, zb, gb, yb, wu, wd, save)
    outs.start(yb, y_out)
    cy.wait()
    ff_backward(gains, dyb, gb, mb, accb, dmb, dmlb, nothing, wu, wd, nothing, nothing)
    attention_backward(gains, mask, dmb, dmlb, invb, donb, dvtb, 0, accb, xb, dx_out, table, wv, wo, nothing)
    outs.wait()


def both_row(row, flag, seg, gains, tok, recv, cot, weights):
    width, ff, heads = tok.shape[1], weights[3].shape[1], weights[0].shape[0]
    V = pltpu.VMEM
    wide = lambda dt: pltpu.HBM((L, width), dt)
    one = V((L, width), bf16)
    big = V((L, width), f32)
    full = V((L, ff), bf16)
    out_shape = [wide(bf16), one] + [wide(bf16)] * 3 + [wide(f32), wide(bf16), wide(f32)]
    out_shape += [pltpu.HBM((L, ff), bf16), wide(bf16), pltpu.HBM((L, ff), bf16)]
    got = pl.pallas_call(
        functools.partial(both_kernel, row),
        out_shape=out_shape,
        in_specs=[SMEM, WHOLE, WHOLE] + [ANY] * 3 + [WHOLE] * 5,
        out_specs=[ANY, WHOLE] + [ANY] * (len(out_shape) - 2),
        scratch_shapes=[one, V((L, L), bf16), one, one, one, one, one, one, big, full, big, full]
        + [one, big, big, one, one, V((width, L), bf16)]
        + [pltpu.SemaphoreType.DMA((4,)), pltpu.SemaphoreType.DMA((20,))],
        **params(28, 2 * L * width * (2 * width + 2 * ff) + 3 * heads * L * L * 128, "forward_backward"),
    )(flag, seg, gains, *far([tok]), recv, *far([cot]), *hold(weights))
    return got[0], got[1], dict(zip(RES, got[2:]))


def ring_place(zy, zs):
    z, y = zy // 2, zy % 2
    return z if y == 0 else 2 * zs - 1 - z


def put_halves(core, block, keep, send, at):
    half = block.shape[0] // 2
    top, bottom = block[:half], block[half:]
    keep[at] = jnp.where(core == 0, top, bottom).astype(keep.dtype)
    send[at] = jnp.where(core == 0, bottom, top).astype(send.dtype)


def turn_into(zs, core, total, turned, base):
    def put(first, part):
        t = part.T
        if zs is None:
            turned[0][base + first : base + first + t.shape[0], :] = t
            return
        pair = total // (2 * zs)
        for s in range(t.shape[0] // pair):
            row = base + ring_place(first // pair + s, zs) * (pair // 2)
            put_halves(core, t[s * pair : (s + 1) * pair], turned[0], turned[1], slice(row, row + pair // 2))

    return put


def backward_kernel(zs, row, part, *refs):
    it = iter(refs)
    take = lambda n: [next(it) for _ in range(n)]
    n_turn = 1 if zs is None else 2
    flag, gains, cot, recv, wu, wd, m, g = take(8)
    if part == 0:
        seg, table, wv, wo, x, inv = take(6)
    hidden = take(n_turn)
    outer = take(n_turn) if part else hidden
    dml_out, dm_out, dg_out = take(3)
    if part == 0:
        don_out, dvt_out = take(2)
    dyb, accb, rb = take(3)
    if part == 0:
        gb, mb, dmlb, mask, invb, xb, donb, dvtb = take(8)
        dmb = mb
    else:
        gb, mb, dmlb, dmb = g, take(1)[0], dml_out, dm_out
    sin, sout = take(2)
    width, ff = dyb.shape[1], gb.shape[1]
    is_enc = flag[0]
    ins, outs = Copies(sin), Copies(sout)
    cy = ins.start(cot.at[pl.ds(row * L, L)], dyb)
    cr = ins.start(recv, rb)
    if part:
        before = [nothing, ins.start(m, mb).wait]
    else:
        before = [ins.start(g, gb).wait, ins.start(m, mb).wait]
        ci, cx = ins.start(inv, invb), ins.start(x, xb)
        build_mask(seg[row : row + 1, :].astype(f32), is_enc, mask)
    cy.wait()
    cr.wait()
    dyb[...] = jnp.where(is_enc == 1, rb[...], dyb[...])
    put = turn_into(zs, flag[1], ff, hidden, 0)
    turn_into(zs, flag[1], width, outer, 0 if part else ff // n_turn)(0, dyb[...])
    dg2 = ff_backward(gains, dyb, gb, mb, accb, dmb, dmlb, put, wu, wd, *before)
    dg1 = jnp.zeros_like(dg2)
    if part == 0:
        ci.wait()
        cx.wait()
        dg1 = attention_backward(gains, mask, mb, dmlb, invb, donb, dvtb, 0, accb, xb, mb, table, wv, wo, nothing)
        outs.start(dmlb, dml_out)
        outs.start(donb, don_out)
        outs.start(dvtb, dvt_out)
        outs.start(dmb, dm_out)
    dg_out[0:1, :] = dg1
    dg_out[1:2, :] = dg2
    outs.wait()


def backward_row(zs, row, flag, seg, gains, cot, recv, weights, res, part):
    width, ff, heads = cot.shape[1], weights[3].shape[1], weights[0].shape[0]
    V = pltpu.VMEM
    wide = lambda dt: pltpu.HBM((L, width), dt)
    n_turn = 1 if zs is None else 2
    tall = [V((n // n_turn, L), bf16) for n in ((ff, width) if part else (ff + width,)) for _ in range(n_turn)]
    one, big, full = V((L, width), bf16), V((L, width), f32), V((L, ff), bf16)
    out_shape = tall + ([one, big] if part else [wide(bf16), wide(f32)]) + [sds((2, width), f32)]
    out_specs = [WHOLE] * len(tall) + [WHOLE if part else ANY] * 2 + [WHOLE]
    scratch = [one, big, one]
    ins = [flag, gains, *far([cot]), recv, *hold(weights[3:]), *far([res["m"]]), *(hold if part else far)([res["g"]])]
    specs = [SMEM, WHOLE, ANY, ANY, WHOLE, WHOLE, ANY, WHOLE if part else ANY]
    if part:
        scratch.append(big)
    names = ["hidden", "send_hidden", "outer", "send_outer"]
    names = [n for n in names if (part or "outer" not in n) and (zs or "send" not in n)] + ["dml", "dm", "dg"]
    if part == 0:
        out_shape += [wide(bf16), pltpu.HBM((width, L), bf16)]
        out_specs += [ANY, ANY]
        names += ["don", "dvt"]
        scratch += [full, big, one, V((L, L), bf16), big, one, one, V((width, L), bf16)]
        ins += [seg, *hold(weights[:3]), *far([res["x"], res["inv"]])]
        specs += [WHOLE] * 4 + [ANY, ANY]
    macs = 2 * L * width * ff + (0 if part else 2 * L * width * width + 2 * heads * L * L * 64)
    got = pl.pallas_call(
        functools.partial(backward_kernel, zs, row, part),
        out_shape=out_shape,
        in_specs=specs,
        out_specs=out_specs,
        scratch_shapes=scratch + [pltpu.SemaphoreType.DMA((8,)), pltpu.SemaphoreType.DMA((8,))],
        **params(8 if part else 16, macs, "ff_backward" if part else "backward"),
    )(*ins)
    return dict(zip(names, got))


def down_kernel(zs, count, *refs):
    turned, z = refs[:count], refs[count : 2 * count]
    out, left, right, stage, sin, sout = refs[2 * count :]
    ins, outs = Copies(sin), Copies(sout)
    ff, step = right.shape[1], stage.shape[-1] if zs else left.shape[0]
    chunks = [(0, step // 2), (step // 2, step // 2)] + [(k * step, step) for k in range(1, ff // step)]
    waits = []
    for at, size in chunks:
        lanes = pl.ds(at, size)
        waits.append([ins.start(a.at[:, lanes], right.at[pl.ds(r * L, L), lanes]) for r, a in enumerate(z)])
    for r, t in enumerate(turned):
        left[:, r * L : (r + 1) * L] = t[t.shape[0] - left.shape[0] :, :]
    for (at, size), some in zip(chunks, waits):
        for c in some:
            c.wait()
        got = dot(left[...], right[:, at : at + size], 1, 0).astype(bf16)
        if zs is None:
            where = (slice(None), pl.ds(at, size))
            stage[:, at : at + size] = got
        else:
            per = got.shape[0] // (2 * zs)
            lane = at % step
            where = (slice(None), pl.ds(at // step * per, per), pl.ds(lane, size))
            stage[:, at // step * per : (at // step + 1) * per, lane : lane + size] = got.reshape(2 * zs, per, size)
        outs.start(stage.at[where], out.at[where])
    outs.wait()


def up_kernel(zs, count, *refs):
    turned, a2 = refs[:count], refs[count : 2 * count]
    out, stage, sout = refs[-3:]
    outs = Copies(sout)
    rows = turned[-1].shape[0]
    parts = 4
    some = rows // parts
    for i in range(parts):
        got = 0.0
        for t, a in zip(turned, a2):
            got = got + dot(t[i * some : (i + 1) * some, :], a[...], 1, 0)
        got = got.astype(bf16)
        if zs is None:
            at = pl.ds(i * some, some)
            stage[at] = got
            outs.start(stage.at[at], out.at[at])
        else:
            n = 2 * zs // parts
            at = pl.ds(i * n, n)
            stage[at] = got.reshape(n, some // n, got.shape[1])
            outs.start(stage.at[at], out.at[at, pl.ds(out.shape[1] // 2, some // n)])
    outs.wait()


def down_grad(zs, turned, z):
    count, ff = len(turned), z[0].shape[1]
    width = turned[-1].shape[0] * (1 if zs is None else 2)
    V = pltpu.VMEM
    if zs is None:
        out, stage = pltpu.HBM((width, ff), bf16), V((width, ff), bf16)
    else:
        out, stage = pltpu.HBM((2 * zs, ff // (2 * zs), width), bf16), V((2 * zs, ff // (4 * zs), width), bf16)
    return pl.pallas_call(
        functools.partial(down_kernel, zs, count),
        out_shape=out,
        in_specs=[WHOLE] * count + [ANY] * count,
        out_specs=ANY,
        scratch_shapes=[V((turned[-1].shape[0], count * L), bf16), V((count * L, ff), bf16), stage]
        + [pltpu.SemaphoreType.DMA((6 * count,)), pltpu.SemaphoreType.DMA((5,))],
        **params(18 if zs else 32, count * L * ff * width // (1 if zs is None else 2), "down_grad"),
    )(*hold(turned), *mixed_far(z))


def up_grad(zs, turned, a2, before=None):
    count, width = len(turned), a2[0].shape[1]
    ff = turned[-1].shape[0] * (1 if zs is None else 2)
    V = pltpu.VMEM
    if zs is None:
        out, stage = pltpu.HBM((ff, width), bf16), V((ff, width), bf16)
    else:
        out, stage = pltpu.HBM((2 * zs, ff // (2 * zs), width), bf16), V((2 * zs, ff // (4 * zs), width), bf16)
    ins = [*hold(turned), *hold(a2)] + ([] if before is None else far([before]))
    return pl.pallas_call(
        functools.partial(up_kernel, zs, count),
        out_shape=out,
        in_specs=[WHOLE] * (2 * count) + ([] if before is None else [ANY]),
        out_specs=ANY,
        input_output_aliases={} if before is None else {2 * count: 0},
        scratch_shapes=[stage, pltpu.SemaphoreType.DMA((4,))],
        **params(6 if zs else 12, count * L * ff * width // (1 if zs is None else 2), "up_grad"),
    )(*ins)


def rest_kernel(zs, *refs):
    it = iter(refs)
    take = lambda n: [next(it) for _ in range(n)]
    flag, seg, gains, table, wv, wo = take(6)
    dm, dml_last, dg2, inv, x, o_last, v_last, a1_last = take(8)
    rows = (len(refs) - 6 - 8 - (4 if zs is None else 3) - 13) // 7
    dml, don, dvt, dg, o, v, a1 = [take(rows) for _ in range(7)]
    outs_w = take(3 if zs is None else 2)
    dx_out = next(it)
    if zs is None:
        gain_out = outs_w[2]
    mask, dmb, dmlb, invb, xb, accb, donb, dvtb, ob, vb, a1b, gainb, sin = take(13)
    is_enc, core = flag[0], flag[1]
    heads, width = table.shape[0], ob.shape[1]
    last = rows * L
    ins = Copies(sin)
    dml_at = lambda r: dmlb.at[pl.ds(r * L, L)]
    early = [ins.start(dml_last, dml_at(rows)), ins.start(inv, invb)]
    mid = [ins.start(dm, dmb), ins.start(x, xb)]
    ready = [ins.start(v_last, vb.at[pl.ds(last, L)]), ins.start(o_last, ob.at[pl.ds(last, L)])]
    for r in range(rows):
        at = pl.ds(r * L, L)
        ready += [ins.start(v[r], vb.at[at]), ins.start(o[r], ob.at[at]), ins.start(don[r], donb.at[at])]
    later = [ins.start(a1_last, a1b.at[pl.ds(last, L)])]
    for r in range(rows):
        at = pl.ds(r * L, L)
        later += [ins.start(dml[r], dmlb.at[at]), ins.start(a1[r], a1b.at[at]), ins.start(dvt[r], dvtb.at[:, at])]
    for r in range(rows + 1):
        build_mask(seg[r : r + 1, :].astype(f32), is_enc, mask.at[r])
    for c in early:
        c.wait()
    mine = mask.at[rows]

    def before_last():
        for c in mid:
            c.wait()

    dg1 = attention_backward(
        gains, mine, dmb, dmlb.at[pl.ds(last, L)], invb, donb, dvtb, last, accb, xb, dmb, table, wv, wo, before_last
    )
    sent = ins.start(dmb, dx_out)
    gainb[...] = jnp.zeros_like(gainb)
    gainb[0:2, :] = dg2[...]
    gainb[0:1, :] = dg1
    for r in range(rows):
        gainb[0:2, :] += dg[r][...]
    for c in ready:
        c.wait()
    lane = lax.broadcasted_iota(jnp.int32, (L, 128), 1)
    low = lane < HD
    one = jnp.ones((L, 128), bf16)
    for p in range(heads // 2):
        cols = slice(p * 128, (p + 1) * 128)
        total = [0.0, 0.0]
        for r in range(rows + 1):
            at = slice(r * L, (r + 1) * L)
            dn, vp = donb[at, cols], vb[at, cols]
            prod = dn.astype(f32) * ob[at, cols].astype(f32)
            for e in range(2):
                own = low if e == 0 else ~low
                delta = jnp.sum(jnp.where(own, prod, 0.0), axis=-1, keepdims=True) * (-1.0 / 32.0)
                high = delta.astype(bf16)
                less = (delta - high.astype(f32)).astype(bf16)
                fill = jnp.where((lane & (HD - 1)) < 32, high, less)
                term = dot(jnp.where(own, dn, fill), jnp.where(own, vp, one), 1, 1) * mask[r].astype(f32)
                total[e] = term if r == 0 else total[e] + term
        for e in range(2):
            h = 2 * p + e
            ds = total[e] * table[h].astype(f32)
            if zs is None:
                outs_w[0][h] = ds
                continue
            per = L // (4 * zs)
            cut = width - L
            pieces = [[(0, 0, 0, L)], [(0, L, 0, cut), (1, 0, cut, L)], [(1, L - cut, 0, L)]][h % 3]
            for s in range(2 * zs):
                block = ds[2 * per * s : 2 * per * (s + 1)]
                for strip, lane_at, a, b in pieces:
                    row_at = ((h // 3) * 2 + strip) * per
                    at = (ring_place(s, zs), slice(row_at, row_at + per), slice(lane_at, lane_at + b - a))
                    put_halves(core, block[:, a:b], outs_w[0], outs_w[1], at)
    for c in later:
        c.wait()
    for i in range(2):
        got = dot(dmlb[...], ob[...], 0, 0) if i == 0 else dot(dvtb[...], a1b[...], 1, 0)
        if zs is None:
            outs_w[1][i] = got.astype(bf16)
            continue
        per = width // (4 * zs)
        base = heads * L * L // (4 * zs * width)
        for s in range(2 * zs):
            at = (ring_place(s, zs), slice(base + i * per, base + (i + 1) * per))
            put_halves(core, got[2 * per * s : 2 * per * (s + 1)], outs_w[0], outs_w[1], at)
    if zs is None:
        gain_out[...] = gainb[0:2, :]
    else:
        for s in range(2 * zs):
            turns = [gainb[...] if d == 0 else pltpu.roll(gainb[...], width - d * per, 1) for d in (2 * s, 2 * s + 1)]
            at = (ring_place(s, zs), slice(base + 2 * per, base + 2 * per + 16))
            put_halves(core, jnp.concatenate(turns, axis=0), outs_w[0], outs_w[1], at)
    sent.wait()


def rest_grads(zs, flag, seg, gains, weights, saved, grads, mid):
    width, heads = saved[0]["x"].shape[1], weights[0].shape[0]
    rows, last = len(grads), saved[-1]
    V = pltpu.VMEM
    one, big = V((L, width), bf16), V((L, width), f32)
    tall = V(((rows + 1) * L, width), bf16)
    if zs is None:
        blocks = [sds((heads, L, L), f32), sds((2, width, width), bf16), sds((2, width), f32)]
    else:
        size = 4 * zs
        blocks = [sds((2 * zs, heads * L * L // (size * width) + 2 * width // size + 16, width), bf16)] * 2
    front = hold([mid["dm"], mid["dml"]]) + [mid["dg"]] + far([last[n] for n in ("inv", "x", "o", "v", "a1")])
    old = saved[:-1]
    back = far(pick(grads, "dml") + pick(grads, "don") + pick(grads, "dvt")) + pick(grads, "dg")
    back += far(pick(old, "o") + pick(old, "v") + pick(old, "a1"))
    specs = [SMEM] + [WHOLE] * 5 + [WHOLE, WHOLE, WHOLE] + [ANY] * 5 + [ANY] * (3 * rows) + [WHOLE] * rows + [ANY] * (3 * rows)
    got = pl.pallas_call(
        functools.partial(rest_kernel, zs),
        out_shape=blocks + [pltpu.HBM((L, width), f32)],
        in_specs=specs,
        out_specs=[WHOLE] * len(blocks) + [ANY],
        scratch_shapes=[V((rows + 1, L, L), bf16), big, tall, big, one, big, tall, V((width, (rows + 1) * L), bf16), tall, tall, tall]
        + [V((16, width), f32), pltpu.SemaphoreType.DMA((10 + 6 * rows,))],
        **params(20 if zs else 40, (rows + 3) * 2 * L * width * width + (rows + 2) * heads * L * L * 128, "rest_grads"),
    )(flag, seg, gains, *hold(weights[:3]), *front, *back)
    return got[:-1], got[-1]


def unpack_kernel(per, rest, mix_out, value_out, out_out, gain_out):
    heads, query, _ = mix_out.shape
    width = rest.shape[1]
    cut = width - L
    for h in range(heads):
        at = (h // 3) * 2 * query
        first, second = slice(at, at + query), slice(at + query, at + 2 * query)
        if h % 3 == 0:
            mix_out[h] = rest[first, 0:L].astype(f32)
        elif h % 3 == 1:
            mix_out[h, :, 0:cut] = rest[first, L:].astype(f32)
            mix_out[h, :, cut:] = rest[second, 0 : L - cut].astype(f32)
        else:
            mix_out[h] = rest[second, L - cut :].astype(f32)
    base = heads * query * L // width
    out_out[...] = rest[base : base + per, :].astype(f32).T
    value_out[...] = rest[base + per : base + 2 * per, :].astype(f32).T
    gain_out[...] = rest[base + 2 * per : base + 2 * per + 16, :].astype(f32)[0:2, 0:per]


def unpack(rest, heads, per, query):
    width = rest.shape[1]
    shapes = [(heads, query, L), (width, per), (width, per), (2, per)]
    return pl.pallas_call(
        functools.partial(unpack_kernel, per),
        out_shape=[sds(s, f32) for s in shapes],
        in_specs=[WHOLE],
        out_specs=[WHOLE] * 4,
        **params(6, 1000, "unpack"),
    )(rest)


def pick(pieces, name):
    return [p[name] for p in pieces]


def rings(zs):
    order = sorted(range(2 * zs), key=lambda s: ring_place(s, zs))
    return [[2 * s + c for s in order] for c in range(2)]


def ring_sum(blocks, size):
    return lax.psum_scatter(blocks, "dp", scatter_dimension=0, tiled=True, axis_index_groups=rings(size // 4))[0]


def shards(tokens, segment_ids, cotangent, norm_gains, mixing, w_value, w_out, w_up, w_down):
    size = lax.axis_size("dp")
    zs = size // 4 if size == 16 else None
    is_enc = (lax.axis_index("section") == 0).astype(jnp.int32)
    core = lax.axis_index("dp").astype(jnp.int32) % 2
    flag = jnp.stack([is_enc, core])
    count = tokens.shape[0] // L
    heads, width, ff = mixing.shape[1], tokens.shape[1], w_up.shape[2]
    seg = segment_ids.reshape(count, L)
    gains = norm_gains[0]
    args = (flag, seg, gains)
    weights = (mixing[0], w_value[0], w_out[0], w_up[0], w_down[0])
    sent, ys, saved, back, dxs, grads = [], [], [], [], [], []
    for r in range(count):
        if r == 0:
            y, weights = forward_row(r, *args, tokens, weights, first=True)
        else:
            y = forward_row(r, *args, tokens, weights)
        sent.append(lax.ppermute(y, "section", [(0, 1)]))
    for r in range(count):
        y, dx, res = both_row(r, *args, tokens, sent[r], cotangent, weights)
        ys.append(y)
        saved.append(res)
        back.append(lax.ppermute(dx, "section", [(1, 0)]))
    swap = lambda a: lax.ppermute(a, "dp", [(d, d ^ 1) for d in range(size)])
    z, a2 = pick(saved, "z"), pick(saved, "a2")
    hidden, outer = [], []
    if zs is not None:
        z, a2, back[0] = lax.optimization_barrier((z, a2, back[0]))
        swapped = [[swap(a) for a in pieces] for pieces in (z, a2)]
    for r in range(count):
        last = r == count - 1
        got = backward_row(zs, r, *args, cotangent, back[r], weights, saved[r], int(last))
        if last:
            outer.append(got["outer"])
            if zs is not None:
                outer.append(swap(got["send_outer"]))
                outer[-1], got["send_hidden"] = lax.optimization_barrier((outer[-1], got["send_hidden"]))
        hidden.append(got["hidden"])
        if zs is not None:
            hidden.append(swap(got["send_hidden"]))
        if not last:
            dxs.append(got["dm"])
            grads.append(got)
            outer = list(hidden)
    if zs is not None:
        z = [p for both in zip(z, swapped[0]) for p in both]
        a2 = [p for both in zip(a2, swapped[1]) for p in both]
    if zs is None:
        wide = [down_grad(zs, outer, z), up_grad(zs, hidden, a2)]
        held = saved
    else:
        wide = up_grad(zs, hidden, a2, down_grad(zs, outer, z))
        held, wide = lax.optimization_barrier((saved, wide))
    rest, dx = rest_grads(zs, *args, weights, held, grads, got)
    dxs.append(dx)
    per = width // size
    if zs is None:
        scatter = lambda g, at: lax.psum_scatter(g.astype(f32), "dp", scatter_dimension=at, tiled=True)
        down_g = scatter(wide[0], 0).T
        up_g = scatter(wide[1], 0).T
        out_g = scatter(rest[1][0], 0).T
        value_g = scatter(rest[1][1], 0).T
        mix_g = scatter(rest[0], 1)
        gains_g = scatter(rest[2], 1)
    else:
        wide = ring_sum(wide, size)
        cut = ff // size
        down_g = wide[:cut].reshape(ff // width, per, width).transpose(0, 2, 1).reshape(ff, per).astype(f32)
        up_g = wide[cut:].T.astype(f32)
        mix_g, value_g, out_g, gains_g = unpack(ring_sum(rest[0] + swap(rest[1]), size), heads, per, L // size)
    return (
        jnp.concatenate(ys, axis=0)[None],
        jnp.concatenate(dxs, axis=0)[None],
        gains_g[None],
        mix_g[None],
        value_g[None],
        out_g[None],
        up_g[None],
        down_g[None],
    )


def solution(mesh):
    placed = (
        P("dp", None),
        P("dp"),
        P("dp", None),
        P("section", None, None),
        P("section", None, None, None),
        P("section", None, None),
        P("section", None, None),
        P("section", None, None),
        P("section", None, None),
    )
    return jax.shard_map(
        shards,
        mesh=mesh,
        in_specs=placed,
        out_specs=(
            P("section", "dp", None),
            P("section", "dp", None),
            P("section", None, "dp"),
            P("section", None, "dp", None),
            P("section", None, "dp"),
            P("section", None, "dp"),
            P("section", None, "dp"),
            P("section", None, "dp"),
        ),
        check_vma=False,
    )
```

```python
import functools
import jax
import jax.numpy as jnp
from jax import lax
from jax.experimental import pallas as pl
from jax.experimental.pallas import tpu as pltpu
from jax.sharding import PartitionSpec as P

L = 512
HD = 64
eps_norm = 1e-06
bf16 = jnp.bfloat16
f32 = jnp.float32
C0 = 0.7978845608028654
C1 = C0 * 0.044715
RC = 128
MIB = 1024 * 1024
ANY = pl.BlockSpec(memory_space=pl.ANY)
WHOLE = pl.BlockSpec(memory_space=pltpu.VMEM)
SMEM = pl.BlockSpec(memory_space=pltpu.SMEM)
sds = jax.ShapeDtypeStruct


def dot(a, b, ca, cb):
    return lax.dot_general(a, b, (((ca,), (cb,)), ((), ())), preferred_element_type=f32)


def rms_scale(values):
    return lax.rsqrt(jnp.mean(values * values, axis=-1, keepdims=True) + eps_norm)


def gelu_parts(u, want_slope):
    w = u * u
    h = 0.5 + 0.5 * jnp.tanh(u * (C0 + C1 * w))
    if not want_slope:
        return u * h, None
    slope = u * (C0 + (3.0 * C1) * w)
    return u * h, h + (h - h * h) * (slope + slope)


def build_mask(seg, is_enc, mask_ref):
    across = jnp.broadcast_to(seg, (128, L)).T
    for b in range(L // 128):
        same = across == seg[:, b * 128 : (b + 1) * 128]
        pos = lax.broadcasted_iota(jnp.int32, (L, 128), 0)
        key = lax.broadcasted_iota(jnp.int32, (L, 128), 1) + b * 128
        seen = (key <= pos) | (is_enc == 1)
        mask_ref[:, b * 128 : (b + 1) * 128] = jnp.where(same & seen, 1.0, 0.0).astype(bf16)


class Copies:
    def __init__(self, sems):
        self.sems = sems
        self.all = []

    def start(self, src, dst):
        copy = pltpu.make_async_copy(src, dst, self.sems.at[len(self.all)])
        copy.start()
        self.all.append(copy)
        return copy

    def wait(self):
        for copy in self.all:
            copy.wait()


RES = ("x", "a1", "v", "inv", "o", "m", "z", "a2", "g")


def hold(arrays):
    return [pltpu.with_memory_space_constraint(a, pltpu.VMEM) for a in arrays]


def far(arrays):
    return [pltpu.with_memory_space_constraint(a, pltpu.HBM) for a in arrays]


def mixed_far(pieces):
    return [p if i % 2 else far([p])[0] for i, p in enumerate(pieces)]


def attention_forward(gains, mask, xb, a1b, vb, ob, mb, invb, table, wv, wo, save, before_pair, before_out):
    for c in range(L // RC):
        rows = slice(c * RC, (c + 1) * RC)
        xf = xb[rows, :].astype(f32)
        a1b[rows, :] = (xf * rms_scale(xf) * gains[0:1, :]).astype(bf16)
    vb[...] = dot(a1b[...], wv[...], 1, 0).astype(bf16)
    save("a1", a1b)
    save("v", vb)
    low = lax.broadcasted_iota(jnp.int32, (L, 128), 1) < HD
    one = jnp.ones((L, 128), bf16)
    for p in range(table.shape[0] // 2):
        cols = slice(p * 128, (p + 1) * 128)
        before_pair(p)
        vp = vb[:, cols]
        even = dot(table[2 * p] * mask[...], jnp.where(low, vp, one), 1, 0)
        odd = dot(table[2 * p + 1] * mask[...], jnp.where(low, one, vp), 1, 0)
        inv = 1.0 / pltpu.roll(jnp.where(low, odd, even), HD, 1)
        ob[:, cols] = (jnp.where(low, even, odd) * inv).astype(bf16)
        if invb is not None:
            invb[:, cols] = inv
    save("o", ob)
    if invb is not None:
        save("inv", invb)
    before_out()
    mb[...] = xb[...].astype(f32) + dot(ob[...], wo[...], 1, 0)
    save("m", mb)


def ff_forward(gains, mb, a2b, zb, gb, yb, wu, wd, save):
    width, ff = mb.shape[1], wu.shape[1]
    nf = ff // width
    for c in range(L // RC):
        rows = slice(c * RC, (c + 1) * RC)
        m = mb[rows, :]
        a2b[rows, :] = (m * rms_scale(m) * gains[1:2, :]).astype(bf16)
    save("a2", a2b)
    acc = mb[...]
    u = None
    for k in range(nf + 1):
        if k < nf:
            following = dot(a2b[...], wu[:, k * width : (k + 1) * width], 1, 0)
        if k > 0:
            cols = slice((k - 1) * width, k * width)
            z, g = gelu_parts(u, gb is not None)
            z = z.astype(bf16)
            if gb is not None:
                zb[:, cols] = z
                gb[:, cols] = g.astype(bf16)
                part = (slice(None), pl.ds((k - 1) * width, width))
                save("z", zb.at[part], *part)
                save("g", gb.at[part], *part)
            acc = acc + dot(z, wd[cols, :], 1, 0)
        u = following
    yb[...] = acc.astype(bf16)


def norm_back(grad, values, gain):
    scale = rms_scale(values)
    hat = values * scale
    scaled = grad * gain
    back = scale * (scaled - hat * jnp.mean(scaled * hat, axis=-1, keepdims=True))
    return back, jnp.sum(grad * hat, axis=0, keepdims=True)


def ff_backward(gains, span, dyb, gb, mb, accb, dmb, dmlb, put_du, wu, wd, before_slope, before_mid):
    width, ff = dyb.shape[1], wu.shape[1]
    nf = ff // width
    here = slice(*span)
    acc = None
    dz = None
    for k in range(nf + 1):
        if k < nf:
            following = dot(dyb[here, :], wd[k * width : (k + 1) * width, :], 1, 1)
        if k > 0:
            cols = slice((k - 1) * width, k * width)
            if k == 1:
                before_slope()
            part = (dz * gb[here, cols].astype(f32)).astype(bf16)
            put_du((k - 1) * width, part)
            more = dot(part, wu[:, cols], 1, 1)
            acc = more if acc is None else acc + more
        dz = following
    accb[here, :] = acc
    before_mid()
    dg = 0.0
    for c in range(span[0], span[1], RC):
        rows = slice(c, c + RC)
        back, add = norm_back(accb[rows, :], mb[rows, :], gains[1:2, :])
        dg = dg + add
        dm = dyb[rows, :].astype(f32) + back
        dmb[rows, :] = dm
        dmlb[rows, :] = dm.astype(bf16)
    return dg


def attention_backward(gains, span, queries, mask, dmb, dmlb, invb, donb, dvtb, accb, xb, dxb, skip, table, wv, wo):
    here = slice(*span)
    length = span[1] - span[0]
    donb[here, :] = (dot(dmlb[here, :], wo[...], 1, 1) * invb[here, :]).astype(bf16)
    row_at = span[0] // L * L
    seen = (slice(queries[0] - row_at, queries[1] - row_at), slice(span[0] - row_at, span[1] - row_at))
    for p in range(table.shape[0] // 2):
        turned = donb[queries[0] : queries[1], p * 128 : (p + 1) * 128].T
        for e in range(2):
            part = dot(turned[e * HD : (e + 1) * HD], table[(2 * p + e, *seen)] * mask[seen], 1, 0)
            row = p * 128 + e * HD
            dvtb[row : row + HD, here] = part.astype(bf16)
    accb[:length, :] = dot(dvtb[:, here], wv[...], 0, 1)
    dg = 0.0
    for c in range(0, length, RC):
        rows = slice(span[0] + c, span[0] + c + RC)
        back, add = norm_back(accb[c : c + RC, :], xb[rows, :].astype(f32), gains[0:1, :])
        dg = dg + add
        dxb[rows.start - skip : rows.stop - skip, :] = (dmb[rows, :] + back).astype(dxb.dtype)
    return dg


def params(limit, macs, name, moved=20_000_000):
    return dict(
        compiler_params=pltpu.CompilerParams(vmem_limit_bytes=limit * MIB),
        cost_estimate=pl.CostEstimate(flops=10 * macs, bytes_accessed=moved, transcendentals=0),
        name=name,
    )


def nothing(*unused):
    pass


def forward_kernel(first, row, *refs):
    it = iter(refs)
    take = lambda n: [next(it) for _ in range(n)]
    flag, seg, gains, tok = take(4)
    src = take(5)
    y_out = next(it)
    table, wv, wo, wu, wd = take(5) if first else src
    xb, mask, a1b, vb, ob, mb, a2b, sin = take(8)
    width, ff = tok.shape[1], wu.shape[1]
    nf = ff // width
    ins = Copies(sin)
    cx = ins.start(tok.at[pl.ds(row * L, L)], xb)
    if first:
        cv = ins.start(src[1], wv)
        ct = [ins.start(src[0].at[pl.ds(2 * p, 2)], table.at[pl.ds(2 * p, 2)]) for p in range(table.shape[0] // 2)]
        co = ins.start(src[2], wo)
        cu = [ins.start(src[3], wu), ins.start(src[4], wd)]
    build_mask(seg[row : row + 1, :].astype(f32), flag[0], mask)
    cx.wait()

    def before_pair(p):
        if first:
            ct[p].wait()
            for h in (2 * p, 2 * p + 1):
                table[h] = jnp.exp(table[h].astype(f32)).astype(bf16)

    def before_out():
        if first:
            co.wait()
            for c in cu:
                c.wait()

    if first:
        cv.wait()
    attention_forward(gains, mask, xb, a1b, vb, ob, mb, None, table, wv, wo, nothing, before_pair, before_out)
    ff_forward(gains, mb, a2b, None, None, y_out, wu, wd, nothing)


def forward_row(row, flag, seg, gains, tok, weights, first=False):
    width, ff, heads = tok.shape[1], weights[3].shape[1], weights[0].shape[0]
    V = pltpu.VMEM
    out_shape, out_specs = [V((L, width), bf16)], [WHOLE]
    if first:
        out_shape += [V(w.shape, w.dtype) for w in weights]
        out_specs += [WHOLE] * 5
    one = V((L, width), bf16)
    got = pl.pallas_call(
        functools.partial(forward_kernel, first, row),
        out_shape=out_shape,
        in_specs=[SMEM, WHOLE, WHOLE, ANY] + [ANY if first else WHOLE] * 5,
        out_specs=out_specs,
        scratch_shapes=[one, V((L, L), bf16), one, one, one, V((L, width), f32), one, pltpu.SemaphoreType.DMA((16,))],
        **params(9, L * width * (2 * width + 2 * ff) + 2 * heads * L * L * 128, "forward_first" if first else "forward"),
    )(flag, seg, gains, *far([tok]), *(far(weights) if first else hold(weights)))
    return (got[0], got[1:6]) if first else got[0]


def both_kernel(row, begin, *refs):
    it = iter(refs)
    take = lambda n: [next(it) for _ in range(n)]
    flag, seg, gains, tok, recv, cot, table, wv, wo, wu, wd = take(11)
    y_out, dx_out = take(2)
    don_out = next(it) if begin else None
    res = dict(zip(RES, take(len(RES))))
    xb, mask, a1b, vb, ob, a2b, yb, rb, invb, zb = take(10)
    mb, gb = take(2)
    dyb, accb, dmb, dmlb, donb, dvtb, sin, sout = take(8)
    ins, outs = Copies(sin), Copies(sout)

    def save(name, src_ref, *where):
        dst = res[name]
        outs.start(src_ref, dst.at[where] if where else dst)

    cr = ins.start(recv, rb)
    cx = ins.start(tok.at[pl.ds(row * L, L)], xb)
    cy = ins.start(cot.at[pl.ds(row * L, L)], dyb)
    is_enc = flag[0]
    build_mask(seg[row : row + 1, :].astype(f32), is_enc, mask)
    cx.wait()
    cr.wait()
    xb[...] = jnp.where(is_enc == 1, xb[...], rb[...])
    save("x", xb)
    attention_forward(gains, mask, xb, a1b, vb, ob, mb, invb, table, wv, wo, save, nothing, nothing)
    ff_forward(gains, mb, a2b, zb, gb, yb, wu, wd, save)
    outs.start(yb, y_out)
    cy.wait()
    span = (begin, L)
    ff_backward(gains, span, dyb, gb, mb, accb, dmb, dmlb, nothing, wu, wd, nothing, nothing)
    attention_backward(gains, span, span, mask, dmb, dmlb, invb, donb, dvtb, accb, xb, dx_out, begin, table, wv, wo)
    if begin:
        outs.start(donb.at[pl.ds(begin, L - begin)], don_out)
    outs.wait()


def front_kernel(row, end, *refs):
    it = iter(refs)
    take = lambda n: [next(it) for _ in range(n)]
    flag, seg, gains, cot, don, table, wv, wo, wu, wd, x, inv, m, g = take(14)
    dx_out = next(it)
    dyb, gb, mb, invb, xb, accb, dmlb, donb, dvtb, mask, sin = take(11)
    ins = Copies(sin)
    some = pl.ds(0, end)
    cy = ins.start(cot.at[pl.ds(row * L, end)], dyb)
    cg, cm = ins.start(g.at[some], gb), ins.start(m.at[some], mb)
    late = [ins.start(inv.at[some], invb), ins.start(x.at[some], xb), ins.start(don, donb.at[pl.ds(end, L - end)])]
    build_mask(seg[row : row + 1, :].astype(f32), flag[0], mask)
    cy.wait()
    span = (0, end)
    ff_backward(gains, span, dyb, gb, mb, accb, mb, dmlb, nothing, wu, wd, cg.wait, cm.wait)
    for c in late:
        c.wait()
    attention_backward(gains, span, (0, L), mask, mb, dmlb, invb, donb, dvtb, accb, xb, dx_out, 0, table, wv, wo)


def front_row(row, end, flag, seg, gains, cot, don, weights, res):
    width, ff, heads = cot.shape[1], weights[3].shape[1], weights[0].shape[0]
    V = pltpu.VMEM
    one, big = V((end, width), bf16), V((end, width), f32)
    return pl.pallas_call(
        functools.partial(front_kernel, row, end),
        out_shape=one,
        in_specs=[SMEM, WHOLE, WHOLE, ANY, ANY] + [WHOLE] * 5 + [ANY] * 4,
        out_specs=WHOLE,
        scratch_shapes=[one, V((end, ff), bf16), big, big, one, big, one, V((L, width), bf16), V((width, end), bf16)]
        + [V((L, L), bf16), pltpu.SemaphoreType.DMA((6,))],
        **params(12, end * width * (2 * width + 2 * ff) + heads * L * end * 64, "front_backward"),
    )(flag, seg, gains, *far([cot, don]), *hold(weights), *far([res[n] for n in ("x", "inv", "m", "g")]))


def both_row(row, begin, flag, seg, gains, tok, recv, cot, weights):
    width, ff, heads = tok.shape[1], weights[3].shape[1], weights[0].shape[0]
    V = pltpu.VMEM
    wide = lambda dt: pltpu.HBM((L, width), dt)
    one = V((L, width), bf16)
    big = V((L, width), f32)
    full = V((L, ff), bf16)
    out_shape = [wide(bf16), V((L - begin, width), bf16)]
    if begin:
        out_shape.append(pltpu.HBM((L - begin, width), bf16))
    out_shape += [wide(bf16)] * 3 + [wide(f32), wide(bf16), wide(f32)]
    out_shape += [pltpu.HBM((L, ff), bf16), wide(bf16), pltpu.HBM((L, ff), bf16)]
    got = pl.pallas_call(
        functools.partial(both_kernel, row, begin),
        out_shape=out_shape,
        in_specs=[SMEM, WHOLE, WHOLE] + [ANY] * 3 + [WHOLE] * 5,
        out_specs=[ANY, WHOLE] + [ANY] * (len(out_shape) - 2),
        scratch_shapes=[one, V((L, L), bf16), one, one, one, one, one, one, big, full, big, full]
        + [one, big, big, one, one, V((width, L), bf16)]
        + [pltpu.SemaphoreType.DMA((4,)), pltpu.SemaphoreType.DMA((20,))],
        **params(28, 2 * L * width * (2 * width + 2 * ff) + 3 * heads * L * L * 128, "forward_backward"),
    )(flag, seg, gains, *far([tok]), recv, *far([cot]), *hold(weights))
    return got[0], got[1], got[2], dict(zip(RES, got[-len(RES) :]))


def ring_place(zy, zs):
    z, y = zy // 2, zy % 2
    return z if y == 0 else 2 * zs - 1 - z


def put_halves(core, block, keep, send, at):
    half = block.shape[0] // 2
    top, bottom = block[:half], block[half:]
    keep[at] = jnp.where(core == 0, top, bottom).astype(keep.dtype)
    send[at] = jnp.where(core == 0, bottom, top).astype(send.dtype)


def turn_into(zs, core, total, turned, base):
    def put(first, part):
        t = part.T
        if zs is None:
            turned[0][base + first : base + first + t.shape[0], :] = t
            return
        pair = total // (2 * zs)
        for s in range(t.shape[0] // pair):
            row = base + ring_place(first // pair + s, zs) * (pair // 2)
            put_halves(core, t[s * pair : (s + 1) * pair], turned[0], turned[1], slice(row, row + pair // 2))

    return put


def backward_kernel(zs, row, last, pieces, *refs):
    it = iter(refs)
    take = lambda n: [next(it) for _ in range(n)]
    n_turn = 1 if zs is None else 2
    flag, gains, cot = take(3)
    recv = take(pieces)
    wu, wd, m, g = take(4)
    hidden = take(n_turn)
    outer = take(n_turn) if last else hidden
    dml_out, dm_out, dg_out = take(3)
    dyb, accb, rb, mb = take(4)
    gb, dmlb, dmb = (g, dml_out, dm_out) if last else take(2) + [mb]
    sin, sout = take(2)
    width, ff = dyb.shape[1], gb.shape[1]
    ins, outs = Copies(sin), Copies(sout)
    cy = ins.start(cot.at[pl.ds(row * L, L)], dyb)
    cr = []
    for i in range(pieces):
        size = L // pieces
        cr.append(ins.start(recv[i], rb.at[pl.ds(i * size, size)]))
    before_slope = nothing if last else ins.start(g, gb).wait
    before_mid = ins.start(m, mb).wait
    cy.wait()
    for c in cr:
        c.wait()
    dyb[...] = jnp.where(flag[0] == 1, rb[...], dyb[...])
    put = turn_into(zs, flag[1], ff, hidden, 0)
    turn_into(zs, flag[1], width, outer, 0 if last else ff // n_turn)(0, dyb[...])
    dg = ff_backward(gains, (0, L), dyb, gb, mb, accb, dmb, dmlb, put, wu, wd, before_slope, before_mid)
    if not last:
        outs.start(dmlb, dml_out)
        outs.start(dmb, dm_out)
    dg_out[0:1, :] = jnp.zeros_like(dg)
    dg_out[1:2, :] = dg
    outs.wait()


def backward_row(zs, row, last, flag, gains, cot, recv, weights, res):
    width, ff = cot.shape[1], weights[3].shape[1]
    V = pltpu.VMEM
    wide = lambda dt: pltpu.HBM((L, width), dt)
    n_turn = 1 if zs is None else 2
    tall = [V((n // n_turn, L), bf16) for n in ((ff, width) if last else (ff + width,)) for _ in range(n_turn)]
    one, big, full = V((L, width), bf16), V((L, width), f32), V((L, ff), bf16)
    names = ["hidden", "send_hidden", "outer", "send_outer"]
    names = [n for n in names if (last or "outer" not in n) and (zs or "send" not in n)] + ["dml", "dm", "dg"]
    got = pl.pallas_call(
        functools.partial(backward_kernel, zs, row, last, len(recv)),
        out_shape=tall + ([one, big] if last else [wide(bf16), wide(f32)]) + [sds((2, width), f32)],
        in_specs=[SMEM, WHOLE] + [ANY] * (1 + len(recv)) + [WHOLE, WHOLE, ANY, WHOLE if last else ANY],
        out_specs=[WHOLE] * len(tall) + [WHOLE if last else ANY] * 2 + [WHOLE],
        scratch_shapes=[one, big, one, big]
        + ([] if last else [full, one])
        + [pltpu.SemaphoreType.DMA((8,)), pltpu.SemaphoreType.DMA((4,))],
        **params(8 if last else 12, 2 * L * width * ff, "ff_backward"),
    )(flag, gains, *far([cot]), *recv, *hold(weights[3:]), *far([res["m"]]), *(hold if last else far)([res["g"]]))
    return dict(zip(names, got))


def down_kernel(zs, count, *refs):
    turned, z = refs[:count], refs[count : 2 * count]
    out, left, right, stage, sin, sout = refs[2 * count :]
    ins, outs = Copies(sin), Copies(sout)
    ff, step = right.shape[1], stage.shape[-1] if zs else left.shape[0]
    chunks = [(0, step // 2), (step // 2, step // 2)] + [(k * step, step) for k in range(1, ff // step)]
    waits = []
    for at, size in chunks:
        lanes = pl.ds(at, size)
        waits.append([ins.start(a.at[:, lanes], right.at[pl.ds(r * L, L), lanes]) for r, a in enumerate(z)])
    for r, t in enumerate(turned):
        left[:, r * L : (r + 1) * L] = t[t.shape[0] - left.shape[0] :, :]
    for (at, size), some in zip(chunks, waits):
        for c in some:
            c.wait()
        got = dot(left[...], right[:, at : at + size], 1, 0).astype(bf16)
        if zs is None:
            where = (slice(None), pl.ds(at, size))
            stage[:, at : at + size] = got
        else:
            per = got.shape[0] // (2 * zs)
            lane = at % step
            where = (slice(None), pl.ds(at // step * per, per), pl.ds(lane, size))
            stage[:, at // step * per : (at // step + 1) * per, lane : lane + size] = got.reshape(2 * zs, per, size)
        outs.start(stage.at[where], out.at[where])
    outs.wait()


def up_kernel(zs, count, *refs):
    turned, a2 = refs[:count], refs[count : 2 * count]
    out, stage, sout = refs[-3:]
    outs = Copies(sout)
    rows = turned[-1].shape[0]
    parts = 4
    some = rows // parts
    for i in range(parts):
        got = 0.0
        for t, a in zip(turned, a2):
            got = got + dot(t[i * some : (i + 1) * some, :], a[...], 1, 0)
        got = got.astype(bf16)
        if zs is None:
            at = pl.ds(i * some, some)
            stage[at] = got
            outs.start(stage.at[at], out.at[at])
        else:
            n = 2 * zs // parts
            at = pl.ds(i * n, n)
            stage[at] = got.reshape(n, some // n, got.shape[1])
            outs.start(stage.at[at], out.at[at, pl.ds(out.shape[1] // 2, some // n)])
    outs.wait()


def down_grad(zs, turned, z):
    count, ff = len(turned), z[0].shape[1]
    width = turned[-1].shape[0] * (1 if zs is None else 2)
    V = pltpu.VMEM
    if zs is None:
        out, stage = pltpu.HBM((width, ff), bf16), V((width, ff), bf16)
    else:
        out, stage = pltpu.HBM((2 * zs, ff // (2 * zs), width), bf16), V((2 * zs, ff // (4 * zs), width), bf16)
    return pl.pallas_call(
        functools.partial(down_kernel, zs, count),
        out_shape=out,
        in_specs=[WHOLE] * count + [ANY] * count,
        out_specs=ANY,
        scratch_shapes=[V((turned[-1].shape[0], count * L), bf16), V((count * L, ff), bf16), stage]
        + [pltpu.SemaphoreType.DMA((6 * count,)), pltpu.SemaphoreType.DMA((5,))],
        **params(18 if zs else 32, count * L * ff * width // (1 if zs is None else 2), "down_grad"),
    )(*hold(turned), *mixed_far(z))


def up_grad(zs, turned, a2, before=None):
    count, width = len(turned), a2[0].shape[1]
    ff = turned[-1].shape[0] * (1 if zs is None else 2)
    V = pltpu.VMEM
    if zs is None:
        out, stage = pltpu.HBM((ff, width), bf16), V((ff, width), bf16)
    else:
        out, stage = pltpu.HBM((2 * zs, ff // (2 * zs), width), bf16), V((2 * zs, ff // (4 * zs), width), bf16)
    ins = [*hold(turned), *hold(a2)] + ([] if before is None else far([before]))
    return pl.pallas_call(
        functools.partial(up_kernel, zs, count),
        out_shape=out,
        in_specs=[WHOLE] * (2 * count) + ([] if before is None else [ANY]),
        out_specs=ANY,
        input_output_aliases={} if before is None else {2 * count: 0},
        scratch_shapes=[stage, pltpu.SemaphoreType.DMA((4,))],
        **params(6 if zs else 12, count * L * ff * width // (1 if zs is None else 2), "up_grad"),
    )(*ins)


def rest_kernel(zs, *refs):
    it = iter(refs)
    take = lambda n: [next(it) for _ in range(n)]
    flag, seg, gains, table, wv, wo = take(6)
    count = seg.shape[0]
    dml, inv, dm, x, o, v, a1, dg = [take(count) for _ in range(8)]
    outs_w = take(3 if zs is None else 2)
    dx_out = next(it)
    if zs is None:
        gain_out = outs_w[2]
    mask, dmb, dmlb, invb, xb, accb, donb, dvtb, ob, vb, a1b, gainb, sin = take(13)
    is_enc, core = flag[0], flag[1]
    heads, width = table.shape[0], ob.shape[1]
    ins = Copies(sin)
    needed = []
    for r in range(count):
        at = pl.ds(r * L, L)
        needed.append([ins.start(p[r], b.at[at]) for p, b in ((dml, dmlb), (inv, invb), (dm, dmb), (x, xb))])
    ready, later = [], []
    for r in range(count):
        at = pl.ds(r * L, L)
        ready += [ins.start(v[r], vb.at[at]), ins.start(o[r], ob.at[at])]
    for r in range(count):
        later.append(ins.start(a1[r], a1b.at[pl.ds(r * L, L)]))
    for r in range(count):
        build_mask(seg[r : r + 1, :].astype(f32), is_enc, mask.at[r])
    gainb[...] = jnp.zeros_like(gainb)
    sent = []
    for r in range(count):
        for c in needed[r]:
            c.wait()
        span = (r * L, (r + 1) * L)
        dg1 = attention_backward(
            gains, span, span, mask.at[r], dmb, dmlb, invb, donb, dvtb, accb, xb, dmb, 0, table, wv, wo
        )
        sent.append(ins.start(dmb.at[pl.ds(r * L, L)], dx_out.at[pl.ds(r * L, L)]))
        gainb[0:2, :] += dg[r][...]
        gainb[0:1, :] += dg1
    for c in ready:
        c.wait()
    lane = lax.broadcasted_iota(jnp.int32, (L, 128), 1)
    low = lane < HD
    one = jnp.ones((L, 128), bf16)
    for p in range(heads // 2):
        cols = slice(p * 128, (p + 1) * 128)
        total = [0.0, 0.0]
        for r in range(count):
            at = slice(r * L, (r + 1) * L)
            dn, vp = donb[at, cols], vb[at, cols]
            prod = dn.astype(f32) * ob[at, cols].astype(f32)
            for e in range(2):
                own = low if e == 0 else ~low
                delta = jnp.sum(jnp.where(own, prod, 0.0), axis=-1, keepdims=True) * (-1.0 / 32.0)
                high = delta.astype(bf16)
                less = (delta - high.astype(f32)).astype(bf16)
                fill = jnp.where((lane & (HD - 1)) < 32, high, less)
                term = dot(jnp.where(own, dn, fill), jnp.where(own, vp, one), 1, 1) * mask[r].astype(f32)
                total[e] = term if r == 0 else total[e] + term
        for e in range(2):
            h = 2 * p + e
            ds = total[e] * table[h].astype(f32)
            if zs is None:
                outs_w[0][h] = ds
                continue
            per = L // (4 * zs)
            cut = width - L
            pieces = [[(0, 0, 0, L)], [(0, L, 0, cut), (1, 0, cut, L)], [(1, L - cut, 0, L)]][h % 3]
            for s in range(2 * zs):
                block = ds[2 * per * s : 2 * per * (s + 1)]
                for strip, lane_at, a, b in pieces:
                    row_at = ((h // 3) * 2 + strip) * per
                    at = (ring_place(s, zs), slice(row_at, row_at + per), slice(lane_at, lane_at + b - a))
                    put_halves(core, block[:, a:b], outs_w[0], outs_w[1], at)
    for c in later:
        c.wait()
    for i in range(2):
        got = dot(dmlb[...], ob[...], 0, 0) if i == 0 else dot(dvtb[...], a1b[...], 1, 0)
        if zs is None:
            outs_w[1][i] = got.astype(bf16)
            continue
        per = width // (4 * zs)
        base = heads * L * L // (4 * zs * width)
        for s in range(2 * zs):
            at = (ring_place(s, zs), slice(base + i * per, base + (i + 1) * per))
            put_halves(core, got[2 * per * s : 2 * per * (s + 1)], outs_w[0], outs_w[1], at)
    if zs is None:
        gain_out[...] = gainb[0:2, :]
    else:
        for s in range(2 * zs):
            turns = [gainb[...] if d == 0 else pltpu.roll(gainb[...], width - d * per, 1) for d in (2 * s, 2 * s + 1)]
            at = (ring_place(s, zs), slice(base + 2 * per, base + 2 * per + 16))
            put_halves(core, jnp.concatenate(turns, axis=0), outs_w[0], outs_w[1], at)
    for c in sent:
        c.wait()


def rest_grads(zs, flag, seg, gains, weights, saved, grads):
    width, heads, count = saved[0]["x"].shape[1], weights[0].shape[0], len(saved)
    V = pltpu.VMEM
    tall, high = V((count * L, width), bf16), V((count * L, width), f32)
    if zs is None:
        blocks = [sds((heads, L, L), f32), sds((2, width, width), bf16), sds((2, width), f32)]
    else:
        size = 4 * zs
        blocks = [sds((2 * zs, heads * L * L // (size * width) + 2 * width // size + 16, width), bf16)] * 2
    ins, specs = [], []
    for name in ("dml", "inv", "dm", "x", "o", "v", "a1"):
        mine = pick(grads if name in grads[0] else saved, name)
        near = name in ("dml", "dm")
        ins += far(mine[:-1]) + (hold if near else far)(mine[-1:])
        specs += [ANY] * (count - 1) + [WHOLE if near else ANY]
    got = pl.pallas_call(
        functools.partial(rest_kernel, zs),
        out_shape=blocks + [pltpu.HBM((count * L, width), f32)],
        in_specs=[SMEM] + [WHOLE] * 5 + specs + [WHOLE] * count,
        out_specs=[WHOLE] * len(blocks) + [ANY],
        scratch_shapes=[V((count, L, L), bf16), high, tall, high, tall, V((L, width), f32), tall, V((width, count * L), bf16)]
        + [tall, tall, tall, V((16, width), f32), pltpu.SemaphoreType.DMA((8 * count,))],
        **params(26 if zs else 44, count * (4 * L * width * width + 2 * heads * L * L * 128), "rest_grads"),
    )(flag, seg, gains, *hold(weights[:3]), *ins, *pick(grads, "dg"))
    return got[:-1], got[-1]


def unpack_kernel(per, rest, mix_out, value_out, out_out, gain_out):
    heads, query, _ = mix_out.shape
    width = rest.shape[1]
    cut = width - L
    for h in range(heads):
        at = (h // 3) * 2 * query
        first, second = slice(at, at + query), slice(at + query, at + 2 * query)
        if h % 3 == 0:
            mix_out[h] = rest[first, 0:L].astype(f32)
        elif h % 3 == 1:
            mix_out[h, :, 0:cut] = rest[first, L:].astype(f32)
            mix_out[h, :, cut:] = rest[second, 0 : L - cut].astype(f32)
        else:
            mix_out[h] = rest[second, L - cut :].astype(f32)
    base = heads * query * L // width
    out_out[...] = rest[base : base + per, :].astype(f32).T
    value_out[...] = rest[base + per : base + 2 * per, :].astype(f32).T
    gain_out[...] = rest[base + 2 * per : base + 2 * per + 16, :].astype(f32)[0:2, 0:per]


def unpack(rest, heads, per, query):
    width = rest.shape[1]
    shapes = [(heads, query, L), (width, per), (width, per), (2, per)]
    return pl.pallas_call(
        functools.partial(unpack_kernel, per),
        out_shape=[sds(s, f32) for s in shapes],
        in_specs=[WHOLE],
        out_specs=[WHOLE] * 4,
        **params(6, 1000, "unpack"),
    )(rest)


def pick(pieces, name):
    return [p[name] for p in pieces]


def rings(zs):
    order = sorted(range(2 * zs), key=lambda s: ring_place(s, zs))
    return [[2 * s + c for s in order] for c in range(2)]


def ring_sum(blocks, size):
    return lax.psum_scatter(blocks, "dp", scatter_dimension=0, tiled=True, axis_index_groups=rings(size // 4))[0]


def shards(tokens, segment_ids, cotangent, norm_gains, mixing, w_value, w_out, w_up, w_down):
    size = lax.axis_size("dp")
    zs = size // 4 if size == 16 else None
    is_enc = (lax.axis_index("section") == 0).astype(jnp.int32)
    core = lax.axis_index("dp").astype(jnp.int32) % 2
    flag = jnp.stack([is_enc, core])
    count = tokens.shape[0] // L
    heads, width, ff = mixing.shape[1], tokens.shape[1], w_up.shape[2]
    seg = segment_ids.reshape(count, L)
    gains = norm_gains[0]
    args = (flag, seg, gains)
    weights = (mixing[0], w_value[0], w_out[0], w_up[0], w_down[0])
    sent, ys, saved, back, grads = [], [], [], [], []
    for r in range(count):
        if r == 0:
            y, weights = forward_row(r, *args, tokens, weights, first=True)
        else:
            y = forward_row(r, *args, tokens, weights)
        sent.append(lax.ppermute(y, "section", [(0, 1)]))
    for r in range(count):
        begin = L // 2 if r == count - 1 else 0
        y, dx, don, res = both_row(r, begin, *args, tokens, sent[r], cotangent, weights)
        ys.append(y)
        saved.append(res)
        back.append([lax.ppermute(dx, "section", [(1, 0)])])
        if begin:
            dx = front_row(r, begin, *args, cotangent, don, weights, res)
            back[r].insert(0, lax.ppermute(dx, "section", [(1, 0)]))
    swap = lambda a: lax.ppermute(a, "dp", [(d, d ^ 1) for d in range(size)])
    z, a2 = pick(saved, "z"), pick(saved, "a2")
    hidden, outer = [], []
    back[0][0], back[-1][-1] = lax.optimization_barrier((back[0][0], back[-1][-1]))
    if zs is not None:
        z, a2, back[0] = lax.optimization_barrier((z, a2, back[0]))
        swapped = [[swap(a) for a in pieces] for pieces in (z, a2)]
    for r in range(count):
        last = r == count - 1
        got = backward_row(zs, r, last, flag, gains, cotangent, back[r], weights, saved[r])
        grads.append(got)
        if last:
            outer.append(got["outer"])
            if zs is not None:
                outer.append(swap(got["send_outer"]))
                outer[-1], got["send_hidden"] = lax.optimization_barrier((outer[-1], got["send_hidden"]))
        hidden.append(got["hidden"])
        if zs is not None:
            hidden.append(swap(got["send_hidden"]))
        if not last:
            outer = list(hidden)
    if zs is not None:
        z = [p for both in zip(z, swapped[0]) for p in both]
        a2 = [p for both in zip(a2, swapped[1]) for p in both]
    if zs is None:
        wide = [down_grad(zs, outer, z), up_grad(zs, hidden, a2)]
        held = saved
    else:
        wide = up_grad(zs, hidden, a2, down_grad(zs, outer, z))
        held, wide = lax.optimization_barrier((saved, wide))
    rest, dx = rest_grads(zs, *args, weights, held, grads)
    per = width // size
    if zs is None:
        scatter = lambda g, at: lax.psum_scatter(g.astype(f32), "dp", scatter_dimension=at, tiled=True)
        down_g = scatter(wide[0], 0).T
        up_g = scatter(wide[1], 0).T
        out_g = scatter(rest[1][0], 0).T
        value_g = scatter(rest[1][1], 0).T
        mix_g = scatter(rest[0], 1)
        gains_g = scatter(rest[2], 1)
    else:
        wide = ring_sum(wide, size)
        cut = ff // size
        down_g = wide[:cut].reshape(ff // width, per, width).transpose(0, 2, 1).reshape(ff, per).astype(f32)
        up_g = wide[cut:].T.astype(f32)
        mix_g, value_g, out_g, gains_g = unpack(ring_sum(rest[0] + swap(rest[1]), size), heads, per, L // size)
    return (
        jnp.concatenate(ys, axis=0)[None],
        dx[None],
        gains_g[None],
        mix_g[None],
        value_g[None],
        out_g[None],
        up_g[None],
        down_g[None],
    )


def solution(mesh):
    placed = (
        P("dp", None),
        P("dp"),
        P("dp", None),
        P("section", None, None),
        P("section", None, None, None),
        P("section", None, None),
        P("section", None, None),
        P("section", None, None),
        P("section", None, None),
    )
    return jax.shard_map(
        shards,
        mesh=mesh,
        in_specs=placed,
        out_specs=(
            P("section", "dp", None),
            P("section", "dp", None),
            P("section", None, "dp"),
            P("section", None, "dp", None),
            P("section", None, "dp"),
            P("section", None, "dp"),
            P("section", None, "dp"),
            P("section", None, "dp"),
        ),
        check_vma=False,
    )
```

```python
import functools
import jax
import jax.numpy as jnp
from jax import lax
from jax.experimental import pallas as pl
from jax.experimental.pallas import tpu as pltpu
from jax.sharding import PartitionSpec as P

L = 512
HD = 64
eps_norm = 1e-06
bf16 = jnp.bfloat16
f32 = jnp.float32
C0 = 0.7978845608028654
C1 = C0 * 0.044715
RC = 128
MIB = 1024 * 1024
ANY = pl.BlockSpec(memory_space=pl.ANY)
WHOLE = pl.BlockSpec(memory_space=pltpu.VMEM)
SMEM = pl.BlockSpec(memory_space=pltpu.SMEM)
sds = jax.ShapeDtypeStruct


def dot(a, b, ca, cb):
    return lax.dot_general(a, b, (((ca,), (cb,)), ((), ())), preferred_element_type=f32)


def rms_scale(values):
    return lax.rsqrt(jnp.mean(values * values, axis=-1, keepdims=True) + eps_norm)


def gelu_parts(u, want_slope):
    w = u * u
    h = 0.5 + 0.5 * jnp.tanh(u * (C0 + C1 * w))
    if not want_slope:
        return u * h, None
    slope = u * (C0 + (3.0 * C1) * w)
    return u * h, h + (h - h * h) * (slope + slope)


def build_mask(seg, is_enc, mask_ref):
    across = jnp.broadcast_to(seg, (128, L)).T
    for b in range(L // 128):
        same = across == seg[:, b * 128 : (b + 1) * 128]
        pos = lax.broadcasted_iota(jnp.int32, (L, 128), 0)
        key = lax.broadcasted_iota(jnp.int32, (L, 128), 1) + b * 128
        seen = (key <= pos) | (is_enc == 1)
        mask_ref[:, b * 128 : (b + 1) * 128] = jnp.where(same & seen, 1.0, 0.0).astype(bf16)


class Copies:
    def __init__(self, sems):
        self.sems = sems
        self.all = []

    def start(self, src, dst):
        copy = pltpu.make_async_copy(src, dst, self.sems.at[len(self.all)])
        copy.start()
        self.all.append(copy)
        return copy

    def wait(self):
        for copy in self.all:
            copy.wait()


RES = ("x", "a1", "v", "inv", "o", "m", "z", "a2", "g")


def hold(arrays):
    return [pltpu.with_memory_space_constraint(a, pltpu.VMEM) for a in arrays]


def far(arrays):
    return [pltpu.with_memory_space_constraint(a, pltpu.HBM) for a in arrays]


def mixed_far(pieces):
    return [p if i % 2 else far([p])[0] for i, p in enumerate(pieces)]


def attention_forward(gains, mask, xb, a1b, vb, ob, mb, invb, table, wv, wo, save, before_pair, before_out):
    for c in range(L // RC):
        rows = slice(c * RC, (c + 1) * RC)
        xf = xb[rows, :].astype(f32)
        a1b[rows, :] = (xf * rms_scale(xf) * gains[0:1, :]).astype(bf16)
    vb[...] = dot(a1b[...], wv[...], 1, 0).astype(bf16)
    save("a1", a1b)
    save("v", vb)
    low = lax.broadcasted_iota(jnp.int32, (L, 128), 1) < HD
    one = jnp.ones((L, 128), bf16)
    for p in range(table.shape[0] // 2):
        cols = slice(p * 128, (p + 1) * 128)
        before_pair(p)
        vp = vb[:, cols]
        even = dot(table[2 * p] * mask[...], jnp.where(low, vp, one), 1, 0)
        odd = dot(table[2 * p + 1] * mask[...], jnp.where(low, one, vp), 1, 0)
        inv = 1.0 / pltpu.roll(jnp.where(low, odd, even), HD, 1)
        ob[:, cols] = (jnp.where(low, even, odd) * inv).astype(bf16)
        if invb is not None:
            invb[:, cols] = inv
    save("o", ob)
    if invb is not None:
        save("inv", invb)
    before_out()
    mb[...] = xb[...].astype(f32) + dot(ob[...], wo[...], 1, 0)
    save("m", mb)


def ff_forward(gains, mb, a2b, zb, gb, yb, wu, wd, save):
    width, ff = mb.shape[1], wu.shape[1]
    nf = ff // width
    for c in range(L // RC):
        rows = slice(c * RC, (c + 1) * RC)
        m = mb[rows, :]
        a2b[rows, :] = (m * rms_scale(m) * gains[1:2, :]).astype(bf16)
    save("a2", a2b)
    acc = mb[...]
    u = None
    for k in range(nf + 1):
        if k < nf:
            following = dot(a2b[...], wu[:, k * width : (k + 1) * width], 1, 0)
        if k > 0:
            cols = slice((k - 1) * width, k * width)
            z, g = gelu_parts(u, gb is not None)
            z = z.astype(bf16)
            if gb is not None:
                zb[:, cols] = z
                gb[:, cols] = g.astype(bf16)
                part = (slice(None), pl.ds((k - 1) * width, width))
                save("z", zb.at[part], *part)
                save("g", gb.at[part], *part)
            acc = acc + dot(z, wd[cols, :], 1, 0)
        u = following
    yb[...] = acc.astype(bf16)


def norm_back(grad, values, gain):
    scale = rms_scale(values)
    hat = values * scale
    scaled = grad * gain
    back = scale * (scaled - hat * jnp.mean(scaled * hat, axis=-1, keepdims=True))
    return back, jnp.sum(grad * hat, axis=0, keepdims=True)


def ff_backward(gains, span, dyb, gb, mb, accb, dmb, dmlb, put_du, wu, wd, before_slope, before_mid, before_part=None):
    width, ff = dyb.shape[1], wu.shape[1]
    nf = ff // width
    here = slice(*span)
    acc = None
    dz = None
    for k in range(nf + 1):
        if k < nf:
            if before_part:
                before_part[k].wait()
            following = dot(dyb[here, :], wd[k * width : (k + 1) * width, :], 1, 1)
        if k > 0:
            cols = slice((k - 1) * width, k * width)
            if k == 1:
                before_slope()
            part = (dz * gb[here, cols].astype(f32)).astype(bf16)
            put_du((k - 1) * width, part)
            more = dot(part, wu[:, cols], 1, 1)
            acc = more if acc is None else acc + more
        dz = following
    accb[here, :] = acc
    before_mid()
    dg = 0.0
    for c in range(span[0], span[1], RC):
        rows = slice(c, c + RC)
        back, add = norm_back(accb[rows, :], mb[rows, :], gains[1:2, :])
        dg = dg + add
        dm = dyb[rows, :].astype(f32) + back
        dmb[rows, :] = dm
        dmlb[rows, :] = dm.astype(bf16)
    return dg


def attention_backward(gains, span, queries, mask, dmb, dmlb, invb, donb, dvtb, accb, xb, dxb, skip, table, wv, wo):
    here = slice(*span)
    length = span[1] - span[0]
    donb[here, :] = (dot(dmlb[here, :], wo[...], 1, 1) * invb[here, :]).astype(bf16)
    row_at = span[0] // L * L
    seen = (slice(queries[0] - row_at, queries[1] - row_at), slice(span[0] - row_at, span[1] - row_at))
    for p in range(table.shape[0] // 2):
        turned = donb[queries[0] : queries[1], p * 128 : (p + 1) * 128].T
        for e in range(2):
            part = dot(turned[e * HD : (e + 1) * HD], table[(2 * p + e, *seen)] * mask[seen], 1, 0)
            row = p * 128 + e * HD
            dvtb[row : row + HD, here] = part.astype(bf16)
    accb[:length, :] = dot(dvtb[:, here], wv[...], 0, 1)
    dg = 0.0
    for c in range(0, length, RC):
        rows = slice(span[0] + c, span[0] + c + RC)
        back, add = norm_back(accb[c : c + RC, :], xb[rows, :].astype(f32), gains[0:1, :])
        dg = dg + add
        dxb[rows.start - skip : rows.stop - skip, :] = (dmb[rows, :] + back).astype(dxb.dtype)
    return dg


def params(limit, macs, name, moved=20_000_000):
    return dict(
        compiler_params=pltpu.CompilerParams(vmem_limit_bytes=limit * MIB),
        cost_estimate=pl.CostEstimate(flops=10 * macs, bytes_accessed=moved, transcendentals=0),
        name=name,
    )


def nothing(*unused):
    pass


def forward_kernel(first, row, *refs):
    it = iter(refs)
    take = lambda n: [next(it) for _ in range(n)]
    flag, seg, gains, tok = take(4)
    src = take(5)
    y_out = next(it)
    table, wv, wo, wu, wd = take(5) if first else src
    xb, mask, a1b, vb, ob, mb, a2b, sin = take(8)
    width, ff = tok.shape[1], wu.shape[1]
    nf = ff // width
    ins = Copies(sin)
    cx = ins.start(tok.at[pl.ds(row * L, L)], xb)
    if first:
        cv = ins.start(src[1], wv)
        ct = [ins.start(src[0].at[pl.ds(2 * p, 2)], table.at[pl.ds(2 * p, 2)]) for p in range(table.shape[0] // 2)]
        co = ins.start(src[2], wo)
        cu = [ins.start(src[3], wu), ins.start(src[4], wd)]
    build_mask(seg[row : row + 1, :].astype(f32), flag[0], mask)
    cx.wait()

    def before_pair(p):
        if first:
            ct[p].wait()
            for h in (2 * p, 2 * p + 1):
                table[h] = jnp.exp(table[h].astype(f32)).astype(bf16)

    def before_out():
        if first:
            co.wait()
            for c in cu:
                c.wait()

    if first:
        cv.wait()
    attention_forward(gains, mask, xb, a1b, vb, ob, mb, None, table, wv, wo, nothing, before_pair, before_out)
    ff_forward(gains, mb, a2b, None, None, y_out, wu, wd, nothing)


def forward_row(row, flag, seg, gains, tok, weights, first=False):
    width, ff, heads = tok.shape[1], weights[3].shape[1], weights[0].shape[0]
    V = pltpu.VMEM
    out_shape, out_specs = [V((L, width), bf16)], [WHOLE]
    if first:
        out_shape += [V(w.shape, w.dtype) for w in weights]
        out_specs += [WHOLE] * 5
    one = V((L, width), bf16)
    got = pl.pallas_call(
        functools.partial(forward_kernel, first, row),
        out_shape=out_shape,
        in_specs=[SMEM, WHOLE, WHOLE, ANY] + [ANY if first else WHOLE] * 5,
        out_specs=out_specs,
        scratch_shapes=[one, V((L, L), bf16), one, one, one, V((L, width), f32), one, pltpu.SemaphoreType.DMA((16,))],
        **params(9, L * width * (2 * width + 2 * ff) + 2 * heads * L * L * 128, "forward_first" if first else "forward"),
    )(flag, seg, gains, *far([tok]), *(far(weights) if first else hold(weights)))
    return (got[0], got[1:6]) if first else got[0]


def both_kernel(row, begin, *refs):
    it = iter(refs)
    take = lambda n: [next(it) for _ in range(n)]
    flag, seg, gains, tok, recv, cot, table, wv, wo, wu, wd = take(11)
    y_out, dx_out = take(2)
    don_out = next(it) if begin else None
    res = dict(zip(RES, take(len(RES))))
    xb, mask, a1b, vb, ob, a2b, yb, rb, invb, zb = take(10)
    mb, gb = take(2)
    dyb, accb, dmb, dmlb, donb, dvtb, sin, sout = take(8)
    ins, outs = Copies(sin), Copies(sout)

    def save(name, src_ref, *where):
        dst = res[name]
        outs.start(src_ref, dst.at[where] if where else dst)

    cr = ins.start(recv, rb)
    cx = ins.start(tok.at[pl.ds(row * L, L)], xb)
    cy = ins.start(cot.at[pl.ds(row * L, L)], dyb)
    is_enc = flag[0]
    build_mask(seg[row : row + 1, :].astype(f32), is_enc, mask)
    cx.wait()
    cr.wait()
    xb[...] = jnp.where(is_enc == 1, xb[...], rb[...])
    save("x", xb)
    attention_forward(gains, mask, xb, a1b, vb, ob, mb, invb, table, wv, wo, save, nothing, nothing)
    ff_forward(gains, mb, a2b, zb, gb, yb, wu, wd, save)
    outs.start(yb, y_out)
    cy.wait()
    span = (begin, L)
    ff_backward(gains, span, dyb, gb, mb, accb, dmb, dmlb, nothing, wu, wd, nothing, nothing)
    attention_backward(gains, span, span, mask, dmb, dmlb, invb, donb, dvtb, accb, xb, dx_out, begin, table, wv, wo)
    if begin:
        outs.start(donb.at[pl.ds(begin, L - begin)], don_out)
    outs.wait()


def front_kernel(row, end, *refs):
    it = iter(refs)
    take = lambda n: [next(it) for _ in range(n)]
    flag, seg, gains, cot, don, table, wv, wo, wu, wd, x, inv, m, g = take(14)
    dx_out = next(it)
    dyb, gb, mb, invb, xb, accb, dmlb, donb, dvtb, mask, sin = take(11)
    ins = Copies(sin)
    some = pl.ds(0, end)
    cy = ins.start(cot.at[pl.ds(row * L, end)], dyb)
    cg, cm = ins.start(g.at[some], gb), ins.start(m.at[some], mb)
    late = [ins.start(inv.at[some], invb), ins.start(x.at[some], xb), ins.start(don, donb.at[pl.ds(end, L - end)])]
    build_mask(seg[row : row + 1, :].astype(f32), flag[0], mask)
    cy.wait()
    span = (0, end)
    ff_backward(gains, span, dyb, gb, mb, accb, mb, dmlb, nothing, wu, wd, cg.wait, cm.wait)
    for c in late:
        c.wait()
    attention_backward(gains, span, (0, L), mask, mb, dmlb, invb, donb, dvtb, accb, xb, dx_out, 0, table, wv, wo)


def front_row(row, end, flag, seg, gains, cot, don, weights, res):
    width, ff, heads = cot.shape[1], weights[3].shape[1], weights[0].shape[0]
    V = pltpu.VMEM
    one, big = V((end, width), bf16), V((end, width), f32)
    return pl.pallas_call(
        functools.partial(front_kernel, row, end),
        out_shape=one,
        in_specs=[SMEM, WHOLE, WHOLE, ANY, ANY] + [WHOLE] * 5 + [ANY] * 4,
        out_specs=WHOLE,
        scratch_shapes=[one, V((end, ff), bf16), big, big, one, big, one, V((L, width), bf16), V((width, end), bf16)]
        + [V((L, L), bf16), pltpu.SemaphoreType.DMA((6,))],
        **params(12, end * width * (2 * width + 2 * ff) + heads * L * end * 64, "front_backward"),
    )(flag, seg, gains, *far([cot, don]), *hold(weights), *far([res[n] for n in ("x", "inv", "m", "g")]))


def both_row(row, begin, flag, seg, gains, tok, recv, cot, weights):
    width, ff, heads = tok.shape[1], weights[3].shape[1], weights[0].shape[0]
    V = pltpu.VMEM
    wide = lambda dt: pltpu.HBM((L, width), dt)
    one = V((L, width), bf16)
    big = V((L, width), f32)
    full = V((L, ff), bf16)
    out_shape = [wide(bf16), V((L - begin, width), bf16)]
    if begin:
        out_shape.append(pltpu.HBM((L - begin, width), bf16))
    out_shape += [wide(bf16)] * 3 + [wide(f32), wide(bf16), wide(f32)]
    out_shape += [pltpu.HBM((L, ff), bf16), wide(bf16), pltpu.HBM((L, ff), bf16)]
    got = pl.pallas_call(
        functools.partial(both_kernel, row, begin),
        out_shape=out_shape,
        in_specs=[SMEM, WHOLE, WHOLE] + [ANY] * 3 + [WHOLE] * 5,
        out_specs=[ANY, WHOLE] + [ANY] * (len(out_shape) - 2),
        scratch_shapes=[one, V((L, L), bf16), one, one, one, one, one, one, big, full, big, full]
        + [one, big, big, one, one, V((width, L), bf16)]
        + [pltpu.SemaphoreType.DMA((4,)), pltpu.SemaphoreType.DMA((20,))],
        **params(28, 2 * L * width * (2 * width + 2 * ff) + 3 * heads * L * L * 128, "forward_backward"),
    )(flag, seg, gains, *far([tok]), recv, *far([cot]), *hold(weights))
    return got[0], got[1], got[2], dict(zip(RES, got[-len(RES) :]))


def ring_place(zy, zs):
    z, y = zy // 2, zy % 2
    return z if y == 0 else 2 * zs - 1 - z


def put_halves(core, block, keep, send, at):
    half = block.shape[0] // 2
    top, bottom = block[:half], block[half:]
    keep[at] = jnp.where(core == 0, top, bottom).astype(keep.dtype)
    send[at] = jnp.where(core == 0, bottom, top).astype(send.dtype)


def turn_into(zs, core, total, turned, base):
    def put(first, part):
        t = part.T
        if zs is None:
            turned[0][base + first : base + first + t.shape[0], :] = t
            return
        pair = total // (2 * zs)
        for s in range(t.shape[0] // pair):
            row = base + ring_place(first // pair + s, zs) * (pair // 2)
            put_halves(core, t[s * pair : (s + 1) * pair], turned[0], turned[1], slice(row, row + pair // 2))

    return put


def backward_kernel(zs, row, last, pieces, *refs):
    it = iter(refs)
    take = lambda n: [next(it) for _ in range(n)]
    n_turn = 1 if zs is None else 2
    flag, gains, cot = take(3)
    recv = take(pieces)
    wu, wd, m, g = take(4)
    hidden = take(n_turn)
    outer = take(n_turn) if last else hidden
    dml_out, dm_out, dg_out = take(3)
    dyb, accb, rb, mb = take(4)
    gb = g if last else next(it)
    dmlb, dmb = dml_out, dm_out
    wd_from = wd
    if not last:
        wd = next(it)
    sin = next(it)
    width, ff = dyb.shape[1], gb.shape[1]
    ins = Copies(sin)
    cy = ins.start(cot.at[pl.ds(row * L, L)], dyb)
    cr = []
    for i in range(pieces):
        size = L // pieces
        cr.append(ins.start(recv[i], rb.at[pl.ds(i * size, size)]))
    parts = []
    if not last:
        for k in range(ff // width):
            some = pl.ds(k * width, width)
            parts.append(ins.start(wd_from.at[some], wd.at[some]))
    before_slope = nothing if last else ins.start(g, gb).wait
    before_mid = ins.start(m, mb).wait
    cy.wait()
    for c in cr:
        c.wait()
    dyb[...] = jnp.where(flag[0] == 1, rb[...], dyb[...])
    put = turn_into(zs, flag[1], ff, hidden, 0)
    turn_into(zs, flag[1], width, outer, 0 if last else ff // n_turn)(0, dyb[...])
    dg = ff_backward(gains, (0, L), dyb, gb, mb, accb, dmb, dmlb, put, wu, wd, before_slope, before_mid, parts)
    dg_out[0:1, :] = jnp.zeros_like(dg)
    dg_out[1:2, :] = dg


def backward_row(zs, row, last, flag, gains, cot, recv, weights, res):
    width, ff = cot.shape[1], weights[3].shape[1]
    V = pltpu.VMEM
    n_turn = 1 if zs is None else 2
    tall = [V((n // n_turn, L), bf16) for n in ((ff, width) if last else (ff + width,)) for _ in range(n_turn)]
    one, big, full = V((L, width), bf16), V((L, width), f32), V((L, ff), bf16)
    names = ["hidden", "send_hidden", "outer", "send_outer"]
    names = [n for n in names if (last or "outer" not in n) and (zs or "send" not in n)] + ["dml", "dm", "dg"]
    got = pl.pallas_call(
        functools.partial(backward_kernel, zs, row, last, len(recv)),
        out_shape=tall + [one, big, sds((2, width), f32)],
        in_specs=[SMEM, WHOLE] + [ANY] * (1 + len(recv)) + [WHOLE, WHOLE if last else ANY, ANY, WHOLE if last else ANY],
        out_specs=[WHOLE] * (len(tall) + 3),
        scratch_shapes=[one, big, one, big]
        + ([] if last else [full, V((ff, width), bf16)])
        + [pltpu.SemaphoreType.DMA((10,))],
        **params(8 if last else 17, 2 * L * width * ff, "ff_backward"),
    )(flag, gains, *far([cot]), *recv, *hold(weights[3:4]), *(hold if last else far)(weights[4:]), *far([res["m"]]), *(hold if last else far)([res["g"]]))
    return dict(zip(names, got))


def down_kernel(zs, count, *refs):
    turned, z = refs[:count], refs[count : 2 * count]
    out, left, right, stage, sin, sout = refs[2 * count :]
    ins, outs = Copies(sin), Copies(sout)
    ff, step = right.shape[1], stage.shape[-1] if zs else left.shape[0]
    chunks = [(0, step // 2), (step // 2, step // 2)] + [(k * step, step) for k in range(1, ff // step)]
    waits = []
    for at, size in chunks:
        lanes = pl.ds(at, size)
        waits.append([ins.start(a.at[:, lanes], right.at[pl.ds(r * L, L), lanes]) for r, a in enumerate(z)])
    for r, t in enumerate(turned):
        left[:, r * L : (r + 1) * L] = t[t.shape[0] - left.shape[0] :, :]
    for (at, size), some in zip(chunks, waits):
        for c in some:
            c.wait()
        got = dot(left[...], right[:, at : at + size], 1, 0).astype(bf16)
        if zs is None:
            where = (slice(None), pl.ds(at, size))
            stage[:, at : at + size] = got
        else:
            per = got.shape[0] // (2 * zs)
            lane = at % step
            where = (slice(None), pl.ds(at // step * per, per), pl.ds(lane, size))
            stage[:, at // step * per : (at // step + 1) * per, lane : lane + size] = got.reshape(2 * zs, per, size)
        outs.start(stage.at[where], out.at[where])
    outs.wait()


def up_kernel(zs, count, *refs):
    turned, a2 = refs[:count], refs[count : 2 * count]
    out, stage, sout = refs[-3:]
    outs = Copies(sout)
    rows = turned[-1].shape[0]
    parts = 4
    some = rows // parts
    for i in range(parts):
        got = 0.0
        for t, a in zip(turned, a2):
            got = got + dot(t[i * some : (i + 1) * some, :], a[...], 1, 0)
        got = got.astype(bf16)
        if zs is None:
            at = pl.ds(i * some, some)
            stage[at] = got
            outs.start(stage.at[at], out.at[at])
        else:
            n = 2 * zs // parts
            at = pl.ds(i * n, n)
            stage[at] = got.reshape(n, some // n, got.shape[1])
            outs.start(stage.at[at], out.at[at, pl.ds(out.shape[1] // 2, some // n)])
    outs.wait()


def down_grad(zs, turned, z):
    count, ff = len(turned), z[0].shape[1]
    width = turned[-1].shape[0] * (1 if zs is None else 2)
    V = pltpu.VMEM
    if zs is None:
        out, stage = pltpu.HBM((width, ff), bf16), V((width, ff), bf16)
    else:
        out, stage = pltpu.HBM((2 * zs, ff // (2 * zs), width), bf16), V((2 * zs, ff // (4 * zs), width), bf16)
    return pl.pallas_call(
        functools.partial(down_kernel, zs, count),
        out_shape=out,
        in_specs=[WHOLE] * count + [ANY] * count,
        out_specs=ANY,
        scratch_shapes=[V((turned[-1].shape[0], count * L), bf16), V((count * L, ff), bf16), stage]
        + [pltpu.SemaphoreType.DMA((6 * count,)), pltpu.SemaphoreType.DMA((5,))],
        **params(18 if zs else 32, count * L * ff * width // (1 if zs is None else 2), "down_grad"),
    )(*hold(turned), *mixed_far(z))


def up_grad(zs, turned, a2, before=None):
    count, width = len(turned), a2[0].shape[1]
    ff = turned[-1].shape[0] * (1 if zs is None else 2)
    V = pltpu.VMEM
    if zs is None:
        out, stage = pltpu.HBM((ff, width), bf16), V((ff, width), bf16)
    else:
        out, stage = pltpu.HBM((2 * zs, ff // (2 * zs), width), bf16), V((2 * zs, ff // (4 * zs), width), bf16)
    ins = [*hold(turned), *hold(a2)] + ([] if before is None else far([before]))
    return pl.pallas_call(
        functools.partial(up_kernel, zs, count),
        out_shape=out,
        in_specs=[WHOLE] * (2 * count) + ([] if before is None else [ANY]),
        out_specs=ANY,
        input_output_aliases={} if before is None else {2 * count: 0},
        scratch_shapes=[stage, pltpu.SemaphoreType.DMA((4,))],
        **params(6 if zs else 12, count * L * ff * width // (1 if zs is None else 2), "up_grad"),
    )(*ins)


def rest_kernel(zs, *refs):
    it = iter(refs)
    take = lambda n: [next(it) for _ in range(n)]
    flag, seg, gains, table, wv, wo = take(6)
    count = seg.shape[0]
    dml, inv, dm, x, o, v, a1, dg = [take(count) for _ in range(8)]
    outs_w = take(3 if zs is None else 2)
    dx_out = next(it)
    if zs is None:
        gain_out = outs_w[2]
    mask, dmb, dmlb, invb, xb, accb, donb, dvtb, ob, vb, a1b, gainb, sin = take(13)
    is_enc, core = flag[0], flag[1]
    heads, width = table.shape[0], ob.shape[1]
    ins = Copies(sin)
    needed = []
    for r in range(count):
        at = pl.ds(r * L, L)
        needed.append([ins.start(p[r], b.at[at]) for p, b in ((dml, dmlb), (inv, invb), (dm, dmb), (x, xb))])
    ready, later = [], []
    for r in range(count):
        at = pl.ds(r * L, L)
        ready += [ins.start(v[r], vb.at[at]), ins.start(o[r], ob.at[at])]
    for r in range(count):
        later.append(ins.start(a1[r], a1b.at[pl.ds(r * L, L)]))
    for r in range(count):
        build_mask(seg[r : r + 1, :].astype(f32), is_enc, mask.at[r])
    gainb[...] = jnp.zeros_like(gainb)
    sent = []
    for r in range(count):
        for c in needed[r]:
            c.wait()
        span = (r * L, (r + 1) * L)
        dg1 = attention_backward(
            gains, span, span, mask.at[r], dmb, dmlb, invb, donb, dvtb, accb, xb, dmb, 0, table, wv, wo
        )
        sent.append(ins.start(dmb.at[pl.ds(r * L, L)], dx_out.at[pl.ds(r * L, L)]))
        gainb[0:2, :] += dg[r][...]
        gainb[0:1, :] += dg1
    for c in ready:
        c.wait()
    lane = lax.broadcasted_iota(jnp.int32, (L, 128), 1)
    low = lane < HD
    one = jnp.ones((L, 128), bf16)
    for p in range(heads // 2):
        cols = slice(p * 128, (p + 1) * 128)
        total = [0.0, 0.0]
        for r in range(count):
            at = slice(r * L, (r + 1) * L)
            dn, vp = donb[at, cols], vb[at, cols]
            prod = dn.astype(f32) * ob[at, cols].astype(f32)
            for e in range(2):
                own = low if e == 0 else ~low
                delta = jnp.sum(jnp.where(own, prod, 0.0), axis=-1, keepdims=True) * (-1.0 / 32.0)
                high = delta.astype(bf16)
                less = (delta - high.astype(f32)).astype(bf16)
                fill = jnp.where((lane & (HD - 1)) < 32, high, less)
                term = dot(jnp.where(own, dn, fill), jnp.where(own, vp, one), 1, 1) * mask[r].astype(f32)
                total[e] = term if r == 0 else total[e] + term
        for e in range(2):
            h = 2 * p + e
            ds = total[e] * table[h].astype(f32)
            if zs is None:
                outs_w[0][h] = ds
                continue
            per = L // (4 * zs)
            cut = width - L
            pieces = [[(0, 0, 0, L)], [(0, L, 0, cut), (1, 0, cut, L)], [(1, L - cut, 0, L)]][h % 3]
            for s in range(2 * zs):
                block = ds[2 * per * s : 2 * per * (s + 1)]
                for strip, lane_at, a, b in pieces:
                    row_at = ((h // 3) * 2 + strip) * per
                    at = (ring_place(s, zs), slice(row_at, row_at + per), slice(lane_at, lane_at + b - a))
                    put_halves(core, block[:, a:b], outs_w[0], outs_w[1], at)
    for c in later:
        c.wait()
    for i in range(2):
        got = dot(dmlb[...], ob[...], 0, 0) if i == 0 else dot(dvtb[...], a1b[...], 1, 0)
        if zs is None:
            outs_w[1][i] = got.astype(bf16)
            continue
        per = width // (4 * zs)
        base = heads * L * L // (4 * zs * width)
        for s in range(2 * zs):
            at = (ring_place(s, zs), slice(base + i * per, base + (i + 1) * per))
            put_halves(core, got[2 * per * s : 2 * per * (s + 1)], outs_w[0], outs_w[1], at)
    if zs is None:
        gain_out[...] = gainb[0:2, :]
    else:
        for s in range(2 * zs):
            turns = [gainb[...] if d == 0 else pltpu.roll(gainb[...], width - d * per, 1) for d in (2 * s, 2 * s + 1)]
            at = (ring_place(s, zs), slice(base + 2 * per, base + 2 * per + 16))
            put_halves(core, jnp.concatenate(turns, axis=0), outs_w[0], outs_w[1], at)
    for c in sent:
        c.wait()


def rest_grads(zs, flag, seg, gains, weights, saved, grads):
    width, heads, count = saved[0]["x"].shape[1], weights[0].shape[0], len(saved)
    V = pltpu.VMEM
    tall, high = V((count * L, width), bf16), V((count * L, width), f32)
    if zs is None:
        blocks = [sds((heads, L, L), f32), sds((2, width, width), bf16), sds((2, width), f32)]
    else:
        size = 4 * zs
        blocks = [sds((2 * zs, heads * L * L // (size * width) + 2 * width // size + 16, width), bf16)] * 2
    ins, specs = [], []
    for name in ("dml", "inv", "dm", "x", "o", "v", "a1"):
        mine = pick(grads if name in grads[0] else saved, name)
        near = name in ("dml", "dm")
        ins += mine if near else far(mine)
        specs += [ANY] * count
    got = pl.pallas_call(
        functools.partial(rest_kernel, zs),
        out_shape=blocks + [pltpu.HBM((count * L, width), f32)],
        in_specs=[SMEM] + [WHOLE] * 5 + specs + [WHOLE] * count,
        out_specs=[WHOLE] * len(blocks) + [ANY],
        scratch_shapes=[V((count, L, L), bf16), high, tall, high, tall, V((L, width), f32), tall, V((width, count * L), bf16)]
        + [tall, tall, tall, V((16, width), f32), pltpu.SemaphoreType.DMA((8 * count,))],
        **params(26 if zs else 44, count * (4 * L * width * width + 2 * heads * L * L * 128), "rest_grads"),
    )(flag, seg, gains, *hold(weights[:3]), *ins, *pick(grads, "dg"))
    return got[:-1], got[-1]


def unpack_kernel(per, rest, mix_out, value_out, out_out, gain_out):
    heads, query, _ = mix_out.shape
    width = rest.shape[1]
    cut = width - L
    for h in range(heads):
        at = (h // 3) * 2 * query
        first, second = slice(at, at + query), slice(at + query, at + 2 * query)
        if h % 3 == 0:
            mix_out[h] = rest[first, 0:L].astype(f32)
        elif h % 3 == 1:
            mix_out[h, :, 0:cut] = rest[first, L:].astype(f32)
            mix_out[h, :, cut:] = rest[second, 0 : L - cut].astype(f32)
        else:
            mix_out[h] = rest[second, L - cut :].astype(f32)
    base = heads * query * L // width
    out_out[...] = rest[base : base + per, :].astype(f32).T
    value_out[...] = rest[base + per : base + 2 * per, :].astype(f32).T
    gain_out[...] = rest[base + 2 * per : base + 2 * per + 16, :].astype(f32)[0:2, 0:per]


def unpack(rest, heads, per, query):
    width = rest.shape[1]
    shapes = [(heads, query, L), (width, per), (width, per), (2, per)]
    return pl.pallas_call(
        functools.partial(unpack_kernel, per),
        out_shape=[sds(s, f32) for s in shapes],
        in_specs=[WHOLE],
        out_specs=[WHOLE] * 4,
        **params(6, 1000, "unpack"),
    )(rest)


def pick(pieces, name):
    return [p[name] for p in pieces]


def rings(zs):
    order = sorted(range(2 * zs), key=lambda s: ring_place(s, zs))
    return [[2 * s + c for s in order] for c in range(2)]


def ring_sum(blocks, size):
    return lax.psum_scatter(blocks, "dp", scatter_dimension=0, tiled=True, axis_index_groups=rings(size // 4))[0]


def shards(tokens, segment_ids, cotangent, norm_gains, mixing, w_value, w_out, w_up, w_down):
    size = lax.axis_size("dp")
    zs = size // 4 if size == 16 else None
    is_enc = (lax.axis_index("section") == 0).astype(jnp.int32)
    core = lax.axis_index("dp").astype(jnp.int32) % 2
    flag = jnp.stack([is_enc, core])
    count = tokens.shape[0] // L
    heads, width, ff = mixing.shape[1], tokens.shape[1], w_up.shape[2]
    seg = segment_ids.reshape(count, L)
    gains = norm_gains[0]
    args = (flag, seg, gains)
    weights = (mixing[0], w_value[0], w_out[0], w_up[0], w_down[0])
    sent, ys, saved, back, grads = [], [], [], [], []
    for r in range(count):
        if r == 0:
            y, weights = forward_row(r, *args, tokens, weights, first=True)
        else:
            y = forward_row(r, *args, tokens, weights)
        sent.append(lax.ppermute(y, "section", [(0, 1)]))
    for r in range(count):
        begin = L // 2 if r == count - 1 else 0
        y, dx, don, res = both_row(r, begin, *args, tokens, sent[r], cotangent, weights)
        ys.append(y)
        saved.append(res)
        back.append([lax.ppermute(dx, "section", [(1, 0)])])
        if begin:
            dx = front_row(r, begin, *args, cotangent, don, weights, res)
            back[r].insert(0, lax.ppermute(dx, "section", [(1, 0)]))
    swap = lambda a: lax.ppermute(a, "dp", [(d, d ^ 1) for d in range(size)])
    z, a2 = pick(saved, "z"), pick(saved, "a2")
    hidden, outer = [], []
    back[0][0], back[-1][-1] = lax.optimization_barrier((back[0][0], back[-1][-1]))
    if zs is not None:
        z, a2, back[0] = lax.optimization_barrier((z, a2, back[0]))
        swapped = [[swap(a) for a in pieces] for pieces in (z, a2)]
    for r in range(count):
        last = r == count - 1
        own = weights if last else [*weights[:4], w_down[0]]
        got = backward_row(zs, r, last, flag, gains, cotangent, back[r], own, saved[r])
        grads.append(got)
        if last:
            outer.append(got["outer"])
            if zs is not None:
                outer.append(swap(got["send_outer"]))
                outer[-1], got["send_hidden"] = lax.optimization_barrier((outer[-1], got["send_hidden"]))
        hidden.append(got["hidden"])
        if zs is not None:
            hidden.append(swap(got["send_hidden"]))
        if not last:
            outer = list(hidden)
    if zs is not None:
        z = [p for both in zip(z, swapped[0]) for p in both]
        a2 = [p for both in zip(a2, swapped[1]) for p in both]
    if zs is None:
        wide = [down_grad(zs, outer, z), up_grad(zs, hidden, a2)]
        held = saved
    else:
        wide = up_grad(zs, hidden, a2, down_grad(zs, outer, z))
        held, wide = lax.optimization_barrier((saved, wide))
    rest, dx = rest_grads(zs, *args, weights, held, grads)
    per = width // size
    if zs is None:
        scatter = lambda g, at: lax.psum_scatter(g.astype(f32), "dp", scatter_dimension=at, tiled=True)
        down_g = scatter(wide[0], 0).T
        up_g = scatter(wide[1], 0).T
        out_g = scatter(rest[1][0], 0).T
        value_g = scatter(rest[1][1], 0).T
        mix_g = scatter(rest[0], 1)
        gains_g = scatter(rest[2], 1)
    else:
        wide = ring_sum(wide, size)
        cut = ff // size
        down_g = wide[:cut].reshape(ff // width, per, width).transpose(0, 2, 1).reshape(ff, per).astype(f32)
        up_g = wide[cut:].T.astype(f32)
        mix_g, value_g, out_g, gains_g = unpack(ring_sum(rest[0] + swap(rest[1]), size), heads, per, L // size)
    return (
        jnp.concatenate(ys, axis=0)[None],
        dx[None],
        gains_g[None],
        mix_g[None],
        value_g[None],
        out_g[None],
        up_g[None],
        down_g[None],
    )


def solution(mesh):
    placed = (
        P("dp", None),
        P("dp"),
        P("dp", None),
        P("section", None, None),
        P("section", None, None, None),
        P("section", None, None),
        P("section", None, None),
        P("section", None, None),
        P("section", None, None),
    )
    return jax.shard_map(
        shards,
        mesh=mesh,
        in_specs=placed,
        out_specs=(
            P("section", "dp", None),
            P("section", "dp", None),
            P("section", None, "dp"),
            P("section", None, "dp", None),
            P("section", None, "dp"),
            P("section", None, "dp"),
            P("section", None, "dp"),
            P("section", None, "dp"),
        ),
        check_vma=False,
    )
```
